128 devices in a mesh: dp: 8 (over x, z_hi), mp: 16 (over z_lo, y, core).
Axes of the slice: x: 4, y: 4, z: 4 (z_hi: 2, z_lo: 2; z = z_hi * 2 + z_lo), core: 2. Of those that a mesh axis runs over, the one named last changes fastest.
Arguments:
- inputs: bfloat16 [256, 10240], P('dp', 'mp'), may hold values from -6 to 6
- out_grads: bfloat16 [256, 10240], P('dp', 'mp'), may hold values from -6 to 6
- w_in: bfloat16 [10240, 36864], P('mp', 'dp'), may hold values from -0.0625 to 0.0625
- w_out: bfloat16 [36864, 10240], P('dp', 'mp'), may hold values from -0.03125 to 0.03125
Outputs:
- in_grads: float32 [256, 10240], P('dp', 'mp')
- grad_w_in: bfloat16 [10240, 36864], P('mp', 'dp')
- grad_w_out: bfloat16 [36864, 10240], P('dp', 'mp')
The draws below stay inside these ranges and needn't reach their ends.
All inputs are finite; a program needn't handle non-finite values.
Results may differ from the reference program's by a relative error of at most 0.005.
Values may be sent and summed in bfloat16 or wider, within the bound.
A program may use at most 128 MiB of HBM per device.

```python
import math
import jax
import jax.numpy as jnp

D = 10240
FF = 36864
TOKENS = 256


def levels(key, extent, split, least, top_value):
    gain = 1.0
    for axis_at, parts in split:
        draws = jax.random.uniform(jax.random.fold_in(jax.random.fold_in(key, 6), axis_at), (parts,), jnp.float32, least / len(split), top_value / len(split))
        gain = gain * jnp.repeat(jnp.exp(draws), extent[axis_at] // parts).reshape((-1,) + (1,) * (len(extent) - 1 - axis_at))
    return gain


def noise(rng, extent, width, limit, shards=(), kind=jnp.bfloat16):
    drawn = width * jax.random.normal(rng, extent, jnp.float32)
    if shards:
        drawn = drawn * levels(rng, extent, shards, -0.22, 0.18)
    return jnp.clip(drawn, -limit, limit).astype(kind)


def setup_inputs(seed: int = 0) -> dict:
    key_of = jax.random.split(jax.random.key(seed), 5)
    return {
        "inputs": noise(key_of[0], (TOKENS, D), 1.0, 6.0, ((0, 8), (1, 16))),
        "out_grads": noise(key_of[1], (TOKENS, D), 1.0, 6.0, ((0, 8), (1, 16))),
        "w_in": noise(key_of[2], (D, FF), D ** -0.5, 0.0625, ((0, 16), (1, 8))),
        "w_out": noise(key_of[3], (FF, D), FF ** -0.5, 0.03125, ((0, 8), (1, 16))),
    }


def gelu_parts(preact):
    cumul = 0.5 * (1.0 + jax.scipy.special.erf(preact * (1.0 / math.sqrt(2.0))))
    density = jnp.exp(-0.5 * preact * preact) * (1.0 / math.sqrt(2.0 * math.pi))
    return (preact * cumul, cumul + preact * density)

def reference(inputs, out_grads, w_in, w_out):
    preact = jnp.dot(inputs, w_in, preferred_element_type=jnp.float32)
    grad_act = jnp.dot(out_grads, w_out.T, preferred_element_type=jnp.float32)
    gelu_value, gelu_slope = gelu_parts(preact)
    activation = gelu_value.astype(jnp.bfloat16)
    grad_preact = (grad_act * gelu_slope).astype(jnp.bfloat16)
    in_grads = jnp.dot(grad_preact, w_in.T, preferred_element_type=jnp.float32)
    factor = 1.0 / math.sqrt(TOKENS)
    grad_w_in = (jnp.dot(inputs.T, grad_preact, preferred_element_type=jnp.float32) * factor).astype(jnp.bfloat16)
    grad_w_out = (jnp.dot(activation.T, out_grads, preferred_element_type=jnp.float32) * factor).astype(jnp.bfloat16)
    return (in_grads, grad_w_in, grad_w_out)
```

```python
import functools
import math

import jax
import jax.numpy as jnp
from jax import lax
from jax.experimental import pallas as pl
from jax.experimental.pallas import tpu as pltpu
from jax.sharding import PartitionSpec as P

MESH = pl.DeviceIdType.MESH
F32, BF16 = jnp.float32, jnp.bfloat16

NX, NY = 4, 4
GROUPS = 2
LAG1, LAG2, LAG3, LAG4, LAG5, LAG6, LAG7 = 1, 3, 5, 7, 9, 10, 12
SLOTS = 4


def rem(a, b):
    return lax.rem(a, jnp.int32(b))


def div(a, b):
    return lax.div(a, jnp.int32(b))


def mult(v, m):
    return pl.multiple_of(v * m, m)


def dot(a, b):
    return lax.dot_general(a, b, (((1,), (0,)), ((), ())), preferred_element_type=F32)


def dot_nt(a, b):
    return lax.dot_general(a, b, (((1,), (1,)), ((), ())), preferred_element_type=F32)


def dot_tn(a, b):
    return lax.dot_general(a, b, (((0,), (0,)), ((), ())), preferred_element_type=F32)


def gelu_parts(v):
    cumul = 0.5 * (1.0 + lax.erf(v * (1.0 / math.sqrt(2.0))))
    density = jnp.exp(-0.5 * v * v) * (1.0 / math.sqrt(2.0 * math.pi))
    return v * cumul, cumul + v * density


def block_kernel(
    T, D, FC, NF,
    x_hbm, g_hbm, wi_hbm, wo_hbm,
    in_ref, gwi_ref, gwo_ref,
    xg, xt, wi, wo, acc, ag,
    csend, crecv, mine, ysend, yrecv, zmine, zsend, zrecv, dsend, drecv,
    load_sem, wi_sem, wo_sem, a_send, a_recv, i_send, i_recv, d_send, d_recv,
):
    R = NX * T
    H, Q, CB = R // 2, R // 4, FC // NY
    ITEMS = GROUPS * NF
    dp, mp = lax.axis_index("dp"), lax.axis_index("mp")
    x, zhi = div(dp, 2), rem(dp, 2)
    zlo, y, core = div(mp, 8), rem(div(mp, 2), NY), rem(mp, 2)

    def slot_of(j):
        return rem(div(j, 2) + core, 2) * 2 + rem(rem(j, 2) + zlo, 2)

    def mp_peer(dz=0, dy=0, dc=0):
        return (dp, rem(zlo + dz, 2) * 8 + rem(y + dy, NY) * 2 + rem(core + dc, 2))

    def dp_peer(g, k):
        return (rem(x + k, NX) * 2 + rem(zhi + g, 2), mp)

    peers = [mp_peer(dc=1), mp_peer(dz=1)] + [mp_peer(dy=k) for k in range(1, NY)]
    dps = [(g, k) for g in range(GROUPS) for k in range(NX) if g or k]
    barrier = pltpu.get_barrier_semaphore()
    for peer in peers + [dp_peer(g, k) for g, k in dps]:
        pl.semaphore_signal(barrier, inc=1, device_id=peer, device_id_type=MESH)

    own = mult(slot_of(x), T)
    loads = [
        pltpu.make_async_copy(x_hbm, xg.at[0, pl.ds(own, T)], load_sem.at[0]),
        pltpu.make_async_copy(g_hbm, xg.at[1, pl.ds(own, T)], load_sem.at[1]),
    ]
    for c in loads:
        c.start()

    def wi_copy(f):
        cols = pl.ds(mult(f, FC), FC)
        return pltpu.make_async_copy(wi_hbm.at[:, cols], wi.at[:, cols], wi_sem.at[f])

    def wo_copy(f):
        rows = pl.ds(mult(f, FC), FC)
        return pltpu.make_async_copy(wo_hbm.at[rows], wo.at[rows], wo_sem.at[f])

    for f in range(NF):
        wi_copy(f).start()
        wo_copy(f).start()

    def remote(src, dst, send, recv, peer):
        return pltpu.make_async_remote_copy(
            src_ref=src, dst_ref=dst, send_sem=send, recv_sem=recv, device_id=peer, device_id_type=MESH
        )

    def a_copy(i, g, k):
        src = xg.at[:, pl.ds(own, T)]
        dst = xg.at[:, pl.ds(pl.multiple_of(g * R + own, T), T)]
        return remote(src, dst, a_send.at[i], a_recv.at[i], dp_peer(g, k))

    def a_wait(i, g, k):
        land = xg.at[:, pl.ds(pl.multiple_of(g * R + slot_of(rem(x + NX - k, NX)) * T, T), T)]
        remote(land, land, a_send.at[i], a_recv.at[i], dp_peer(g, k)).wait_recv()

    for c in loads:
        c.wait()
    pl.semaphore_wait(barrier, len(peers) + len(dps))
    for i, (g, k) in enumerate(dps):
        a_copy(i, g, k).start()

    def item(t):
        g, f = div(t, NF), rem(t, NF)
        return g, f, pl.multiple_of(g * R, R), pl.multiple_of(f * FC, FC)

    def ycols(base, dy):
        return pl.ds(pl.multiple_of(base + rem(y + dy, NY) * CB, CB), CB)

    def item_copy(t, kind):
        _, _, r0, c0 = item(t)
        name, k = kind
        if name == "c":
            n, src, dst, peer = 0, csend.at[t], crecv.at[t], mp_peer(dc=1)
        elif name == "y":
            n, src, dst, peer = k, ysend.at[t, :, :, ycols(0, k)], yrecv.at[t, k - 1], mp_peer(dy=k)
        elif name == "z":
            n, src, dst, peer = 4, zsend.at[t], zrecv.at[t], mp_peer(dz=1)
        elif name == "Y":
            src = ag.at[:, pl.ds(r0, Q), ycols(c0, 0)]
            n, dst, peer = 4 + k, src, mp_peer(dy=k)
        elif name == "Z":
            n, src, peer = 8, ag.at[:, pl.ds(r0, Q), pl.ds(c0, FC)], mp_peer(dz=1)
            dst = ag.at[:, pl.ds(pl.multiple_of(r0 + Q, Q), Q), pl.ds(c0, FC)]
        else:
            peer = mp_peer(dc=1)
            src = ag.at[:, pl.ds(pl.multiple_of(r0 + k * Q, Q), Q), pl.ds(c0, FC)]
            n, dst = 9 + k, ag.at[:, pl.ds(pl.multiple_of(r0 + H + k * Q, Q), Q), pl.ds(c0, FC)]
        return remote(src, dst, i_send.at[t, n], i_recv.at[t, n], peer)

    def start(t, *kinds):
        for kind in kinds:
            item_copy(t, kind).start()

    def wait_recv(t, *kinds):
        for kind in kinds:
            if kind[0] == "Y":
                _, _, r0, c0 = item(t)
                n = 4 + kind[1]
                land = ag.at[:, pl.ds(r0, Q), ycols(c0, NY - kind[1])]
                remote(land, land, i_send.at[t, n], i_recv.at[t, n], mp_peer(dy=kind[1])).wait_recv()
            else:
                item_copy(t, kind).wait_recv()

    ys = [("y", k) for k in range(1, NY)]
    Ys = [("Y", k) for k in range(1, NY)]

    def stage0(t):
        g, f, r0, c0 = item(t)
        s = rem(t, SLOTS)

        @pl.when(t == 0)
        def _():
            for i, (gg, k) in enumerate(dps):
                if gg == 0:
                    a_wait(i, gg, k)

        @pl.when(t == NF)
        def _():
            for i, (gg, k) in enumerate(dps):
                if gg == 1:
                    a_wait(i, gg, k)
            xt[...] = xg[0].T

        @pl.when(t < NF)
        def _():
            wi_copy(f).wait()
            wo_copy(f).wait()

        pre = dot(xg[0, pl.ds(r0, R)], wi[:, pl.ds(c0, FC)])
        mine[s, 0] = pre[:H]
        csend[t, 0] = pre[H:].astype(BF16)
        grad = dot_nt(xg[1, pl.ds(r0, R)], wo[pl.ds(c0, FC)])
        mine[s, 1] = grad[:H]
        csend[t, 1] = grad[H:].astype(BF16)
        start(t, ("c", 0))

    def stage1(t):
        s = rem(t, SLOTS)
        wait_recv(t, ("c", 0))
        total = mine[s] + crecv[t].astype(F32)
        mine[s] = total
        ysend[t] = total.astype(BF16)
        start(t, *ys)

    def stage2(t):
        s = rem(t, SLOTS)
        wait_recv(t, *ys)
        total = mine[s, :, :, ycols(0, 0)]
        for k in range(NY - 1):
            total = total + yrecv[t, k].astype(F32)
        zmine[s] = total[:, :Q]
        zsend[t] = total[:, Q:].astype(BF16)
        start(t, ("z", 0))

    def stage3(t):
        s = rem(t, SLOTS)
        _, _, r0, c0 = item(t)
        wait_recv(t, ("z", 0))
        total = zmine[s] + zrecv[t].astype(F32)
        value, slope = gelu_parts(total[0])
        ag[0, pl.ds(r0, Q), ycols(c0, 0)] = value.astype(BF16)
        ag[1, pl.ds(r0, Q), ycols(c0, 0)] = (total[1] * slope).astype(BF16)
        start(t, *Ys)

    def stage4(t):
        wait_recv(t, *Ys)
        start(t, ("Z", 0), ("C", 0))

    def stage5(t):
        wait_recv(t, ("Z", 0))
        start(t, ("C", 1))

    def d_copy(i, g, k):
        return remote(dsend.at[i], drecv.at[i], d_send.at[i], d_recv.at[i], dp_peer(g, k))

    def stage6(t):
        g, f, r0, c0 = item(t)
        wait_recv(t, ("C", 0), ("C", 1))
        part = dot_nt(ag[1, pl.ds(r0, R), pl.ds(c0, FC)], wi[:, pl.ds(c0, FC)])

        @pl.when(f == 0)
        def _():
            acc[pl.ds(r0, R)] = part

        @pl.when(f > 0)
        def _():
            acc[pl.ds(r0, R)] += part

        for gg in range(GROUPS):
            @pl.when(t == gg * NF + NF - 1)
            def _():
                for i, (g2, k) in enumerate(dps):
                    if g2 == gg:
                        rows = pl.multiple_of(g2 * R + slot_of(rem(x + k, NX)) * T, T)
                        dsend[i] = acc[pl.ds(rows, T)].astype(BF16)
                        d_copy(i, g2, k).start()

    factor = 1.0 / math.sqrt(GROUPS * R)

    def stage7(t):
        _, _, _, c0 = item(t)
        cols = pl.ds(c0, FC)
        gwi_ref[:, cols] = (dot(xt[...], ag[1, :, cols]) * factor).astype(BF16)
        gwo_ref[cols, :] = (dot_tn(ag[0, :, cols], xg[1]) * factor).astype(BF16)

    stages = [
        (stage5, LAG5, 0), (stage4, LAG4, 0), (stage3, LAG3, 0), (stage2, LAG2, 0), (stage1, LAG1, 0),
        (stage0, 0, 0), (stage6, LAG6, 0), (stage7, LAG7, NF),
    ]

    @pl.loop(0, ITEMS + LAG7)
    def _(tick):
        for stage, lag, first in stages:
            @pl.when(jnp.logical_and(tick >= lag + first, tick < lag + ITEMS))
            def _():
                stage(tick - lag)

    total = acc[pl.ds(own, T)]
    for i, (g, k) in enumerate(dps):
        d_copy(i, g, k).wait_recv()
        total = total + drecv[i].astype(F32)
    in_ref[...] = total

    for i, (g, k) in enumerate(dps):
        a_copy(i, g, k).wait_send()
        d_copy(i, g, k).wait_send()

    @pl.loop(0, ITEMS)
    def _(t):
        for kind in [("c", 0), *ys, ("z", 0), *Ys, ("Z", 0), ("C", 0), ("C", 1)]:
            item_copy(t, kind).wait_send()


def store_kernel(in_ref, gwi_ref, gwo_ref, in_out, gwi_out, gwo_out, sem):
    copies = [
        pltpu.make_async_copy(gwi_ref, gwi_out, sem.at[0]),
        pltpu.make_async_copy(gwo_ref, gwo_out, sem.at[1]),
        pltpu.make_async_copy(in_ref, in_out, sem.at[2]),
    ]
    for c in copies:
        c.start()
    for c in copies:
        c.wait()


def local(inputs, out_grads, w_in, w_out):
    T, D = inputs.shape
    FF = w_in.shape[1]
    FC = 512
    NF = FF // FC
    R = NX * T
    H, Q, CB = R // 2, R // 4, FC // NY
    ITEMS = GROUPS * NF
    TOK = GROUPS * R
    DPS = GROUPS * NX - 1
    vmem = pl.BlockSpec(memory_space=pltpu.VMEM)
    hbm = pl.BlockSpec(memory_space=pl.ANY)
    dma = pltpu.SemaphoreType.DMA
    shapes = [((T, D), F32), ((D, FF), BF16), ((FF, D), BF16)]
    parts = pl.pallas_call(
        functools.partial(block_kernel, T, D, FC, NF),
        out_shape=[pltpu.VMEM(s, d) for s, d in shapes],
        in_specs=[hbm] * 4,
        out_specs=[vmem] * 3,
        scratch_shapes=[
            pltpu.VMEM((2, TOK, D), BF16),
            pltpu.VMEM((D, TOK), BF16),
            pltpu.VMEM((D, FF), BF16),
            pltpu.VMEM((FF, D), BF16),
            pltpu.VMEM((TOK, D), F32),
            pltpu.VMEM((2, TOK, FF), BF16),
            pltpu.VMEM((ITEMS, 2, H, FC), BF16),
            pltpu.VMEM((ITEMS, 2, H, FC), BF16),
            pltpu.VMEM((SLOTS, 2, H, FC), F32),
            pltpu.VMEM((ITEMS, 2, H, FC), BF16),
            pltpu.VMEM((ITEMS, NY - 1, 2, H, CB), BF16),
            pltpu.VMEM((SLOTS, 2, Q, CB), F32),
            pltpu.VMEM((ITEMS, 2, Q, CB), BF16),
            pltpu.VMEM((ITEMS, 2, Q, CB), BF16),
            pltpu.VMEM((DPS, T, D), BF16),
            pltpu.VMEM((DPS, T, D), BF16),
            dma((2,)), dma((NF,)), dma((NF,)),
            dma((DPS,)), dma((DPS,)),
            dma((ITEMS, 11)), dma((ITEMS, 11)),
            dma((DPS,)), dma((DPS,)),
        ],
        compiler_params=pltpu.CompilerParams(
            collective_id=0, has_side_effects=True, vmem_limit_bytes=44 * 2**20
        ),
        name="ffn_backward",
    )(inputs, out_grads, w_in, w_out)
    return pl.pallas_call(
        store_kernel,
        out_shape=[jax.ShapeDtypeStruct(s, d) for s, d in shapes],
        in_specs=[vmem] * 3,
        out_specs=[hbm] * 3,
        scratch_shapes=[dma((3,))],
        compiler_params=pltpu.CompilerParams(vmem_limit_bytes=2**20),
        name="store_results",
    )(*parts)


def solution(mesh):
    return jax.shard_map(
        local,
        mesh=mesh,
        in_specs=(P("dp", "mp"), P("dp", "mp"), P("mp", "dp"), P("dp", "mp")),
        out_specs=(P("dp", "mp"), P("mp", "dp"), P("dp", "mp")),
        check_vma=False,
    )
```

```python
import functools
import math

import jax
import jax.numpy as jnp
from jax import lax
from jax.experimental import pallas as pl
from jax.experimental.pallas import tpu as pltpu
from jax.sharding import PartitionSpec as P

MESH = pl.DeviceIdType.MESH
F32, BF16 = jnp.float32, jnp.bfloat16

NX, NY = 4, 4
GROUPS = 2
LAGS = (0, 3, 8, 13, 18, 22, 26, 30, 32, 34)
SLOTS = 24
ODD_FROM, ODD_TO = 2, 14
NAMES = ("c", "y+", "y-", "r+", "r-", "z", "Z", "Y+", "Y-", "R+", "R-", "C")


def rem(a, b):
    return lax.rem(a, jnp.int32(b))


def div(a, b):
    return lax.div(a, jnp.int32(b))


def mult(v, m):
    return pl.multiple_of(v * m, m)


def dot(a, b):
    return lax.dot_general(a, b, (((1,), (0,)), ((), ())), preferred_element_type=F32)


def dot_nt(a, b):
    return lax.dot_general(a, b, (((1,), (1,)), ((), ())), preferred_element_type=F32)


def dot_tn(a, b):
    return lax.dot_general(a, b, (((0,), (0,)), ((), ())), preferred_element_type=F32)


def gelu_parts(v):
    cumul = 0.5 * (1.0 + lax.erf(v * (1.0 / math.sqrt(2.0))))
    density = jnp.exp(-0.5 * v * v) * (1.0 / math.sqrt(2.0 * math.pi))
    return v * cumul, cumul + v * density


def block_kernel(
    T, D, FC, NF,
    x_hbm, g_hbm, wi_hbm, wo_hbm,
    in_ref, gwi_ref, gwo_ref,
    xg, xt, wi, wo, acc, ag,
    csend, crecv, mine, yp, ym, yq, rp, rm, rq, yown, yrel, zmine, qkeep, zs, zr, dsend, drecv,
    load_sem, wi_sem, wo_sem, a_send, a_recv, i_send, i_recv, d_send, d_recv,
):
    R = NX * T
    H, Q, CB = R // 2, R // 4, FC // NY
    ITEMS = GROUPS * NF
    dp, mp = lax.axis_index("dp"), lax.axis_index("mp")
    x, zhi = div(dp, 2), rem(dp, 2)
    zlo, y, core = div(mp, 8), rem(div(mp, 2), NY), rem(mp, 2)

    def slot_of(j):
        return rem(div(j, 2) + core, 2) * 2 + rem(rem(j, 2) + zlo, 2)

    def mp_peer(dz=0, dy=0, dc=0):
        return (dp, rem(zlo + dz, 2) * 8 + rem(y + dy, NY) * 2 + rem(core + dc, 2))

    def dp_peer(g, k):
        return (rem(x + k, NX) * 2 + rem(zhi + g, 2), mp)

    peers = [mp_peer(dc=1), mp_peer(dz=1)] + [mp_peer(dy=k) for k in range(1, NY)]
    dps = [(g, k) for g in range(GROUPS) for k in range(NX) if g or k]
    barrier = pltpu.get_barrier_semaphore()
    for peer in peers + [dp_peer(g, k) for g, k in dps]:
        pl.semaphore_signal(barrier, inc=1, device_id=peer, device_id_type=MESH)

    own = mult(slot_of(x), T)
    loads = [
        pltpu.make_async_copy(x_hbm, xg.at[0, pl.ds(own, T)], load_sem.at[0]),
        pltpu.make_async_copy(g_hbm, xg.at[1, pl.ds(own, T)], load_sem.at[1]),
    ]
    for c in loads:
        c.start()

    def wi_copy(f):
        cols = pl.ds(mult(f, FC), FC)
        return pltpu.make_async_copy(wi_hbm.at[:, cols], wi.at[:, cols], wi_sem.at[f])

    def wo_copy(f):
        rows = pl.ds(mult(f, FC), FC)
        return pltpu.make_async_copy(wo_hbm.at[rows], wo.at[rows], wo_sem.at[f])

    for f in range(NF):
        wi_copy(f).start()
        wo_copy(f).start()

    def remote(src, dst, send, recv, peer):
        return pltpu.make_async_remote_copy(
            src_ref=src, dst_ref=dst, send_sem=send, recv_sem=recv, device_id=peer, device_id_type=MESH
        )

    def a_copy(i, g, k):
        src = xg.at[:, pl.ds(pl.multiple_of((R if k and g else 0) + own, T), T)]
        dst = xg.at[:, pl.ds(pl.multiple_of(g * R + own, T), T)]
        land = xg.at[:, pl.ds(pl.multiple_of(g * R + slot_of(rem(x + NX - k, NX)) * T, T), T)]
        peer = dp_peer(0, k) if k else dp_peer(g, 0)
        return remote(src, dst, a_send.at[i], a_recv.at[i], peer), remote(land, land, a_send.at[i], a_recv.at[i], peer)

    def gather_start(pick):
        for i, (g, k) in enumerate(dps):
            if pick(g, k):
                a_copy(i, g, k)[0].start()

    def gather_wait(pick):
        for i, (g, k) in enumerate(dps):
            if pick(g, k):
                a_copy(i, g, k)[1].wait_recv()

    for c in loads:
        c.wait()
    pl.semaphore_wait(barrier, len(peers) + len(dps))
    gather_start(lambda g, k: g == 0)
    gather_start(lambda g, k: k == 0)

    def is_odd(t):
        return jnp.logical_and(rem(t, 2) == 0, jnp.logical_and(t >= ODD_FROM, t <= ODD_TO))

    def item(t):
        g, f = div(t, NF), rem(t, NF)
        return g, f, pl.multiple_of(g * R, R), pl.multiple_of(f * FC, FC)

    def ycols(base, dy):
        return pl.ds(pl.multiple_of(base + rem(y + dy, NY) * CB, CB), CB)

    def item_copy(t, odd, name):
        _, _, r0, c0 = item(t)
        rows = Q if odd else H
        n = NAMES.index(name)
        up, down, zp, cp = mp_peer(dy=1), mp_peer(dy=NY - 1), mp_peer(dz=1), mp_peer(dc=1)
        head, own_z, other_z = pl.ds(0, rows), pl.ds(r0, Q), pl.ds(pl.multiple_of(r0 + Q, Q), Q)
        gather = pl.ds(r0, rows)
        zcols = pl.ds(0, FC if odd else CB)
        if name == "c":
            src, dst, peer = csend.at[t], crecv.at[t], cp
        elif name == "y+":
            src, dst, peer = yp.at[t, :, head], rp.at[t, :, head], up
        elif name == "y-":
            src, dst, peer = ym.at[t, :, head], rm.at[t, :, head], down
        elif name == "r+":
            src, dst, peer = yq.at[t, 0, head], rq.at[t, 0, head], up
        elif name == "r-":
            src, dst, peer = yq.at[t, 1, head], rq.at[t, 1, head], down
        elif name == "z":
            src, dst, peer = zs.at[t, :, :, zcols], zr.at[t, :, :, zcols], zp
        elif name == "Z":
            zc = pl.ds(c0, FC) if odd else ycols(c0, 0)
            src, dst, peer = ag.at[:, own_z, zc], ag.at[:, other_z, zc], zp
        elif name == "Y+":
            src, peer = ag.at[:, gather, ycols(c0, 0)], up
            dst, land = src, ag.at[:, gather, ycols(c0, NY - 1)]
        elif name == "Y-":
            src, peer = ag.at[:, gather, ycols(c0, 0)], down
            dst, land = src, ag.at[:, gather, ycols(c0, 1)]
        elif name == "R+":
            src, peer = ag.at[0, gather, ycols(c0, NY - 1)], up
            dst, land = src, ag.at[0, gather, ycols(c0, 2)]
        elif name == "R-":
            src, peer = ag.at[1, gather, ycols(c0, 1)], down
            dst, land = src, ag.at[1, gather, ycols(c0, 2)]
        else:
            src, peer = ag.at[:, pl.ds(r0, H), pl.ds(c0, FC)], cp
            dst = ag.at[:, pl.ds(pl.multiple_of(r0 + H, H), H), pl.ds(c0, FC)]
        if name not in ("Y+", "Y-", "R+", "R-"):
            land = dst
        send, recv = i_send.at[t, n], i_recv.at[t, n]
        return remote(src, dst, send, recv, peer), remote(land, land, send, recv, peer)

    def start(t, odd, *names):
        for name in names:
            item_copy(t, odd, name)[0].start()

    def wait(t, odd, *names):
        for name in names:
            item_copy(t, odd, name)[1].wait_recv()

    def products(t):
        g, f, r0, c0 = item(t)
        s = rem(t, SLOTS)

        @pl.when(t == 0)
        def _():
            gather_wait(lambda g, k: g == 0)

        @pl.when(t == 1)
        def _():
            gather_wait(lambda g, k: k == 0)
            gather_start(lambda g, k: g and k)

        @pl.when(t == NF)
        def _():
            gather_wait(lambda g, k: g and k)
            xt[...] = xg[0].T

        @pl.when(t < NF)
        def _():
            wi_copy(f).wait()
            wo_copy(f).wait()

        pre = dot(xg[0, pl.ds(r0, R)], wi[:, pl.ds(c0, FC)])
        mine[s, 0] = pre[:H]
        csend[t, 0] = pre[H:].astype(BF16)
        grad = dot_nt(xg[1, pl.ds(r0, R)], wo[pl.ds(c0, FC)])
        mine[s, 1] = grad[:H]
        csend[t, 1] = grad[H:].astype(BF16)
        start(t, 0, "c")

    def y_first(t, odd, block):
        s, n = rem(t, SLOTS), Q if odd else H
        yown[s, :, :n] = block(0)
        b = block(1)
        yrel[s, 0, :n] = b[0]
        yp[t, 1, :n] = b[1].astype(BF16)
        b = block(2)
        yp[t, 0, :n] = b[0].astype(BF16)
        start(t, odd, "y+")
        ym[t, 1, :n] = b[1].astype(BF16)
        b = block(3)
        yrel[s, 1, :n] = b[1]
        ym[t, 0, :n] = b[0].astype(BF16)
        start(t, odd, "y-")

    def y_relay(t, odd):
        s, n = rem(t, SLOTS), Q if odd else H
        wait(t, odd, "y+", "y-")
        yq[t, 0, :n] = (yrel[s, 0, :n] + rp[t, 0, :n].astype(F32)).astype(BF16)
        start(t, odd, "r+")
        yq[t, 1, :n] = (yrel[s, 1, :n] + rm[t, 1, :n].astype(F32)).astype(BF16)
        start(t, odd, "r-")
        yown[s, 0, :n] += rm[t, 0, :n].astype(F32)
        yown[s, 1, :n] += rp[t, 1, :n].astype(F32)

    def y_last(t, odd):
        s, n = rem(t, SLOTS), Q if odd else H
        wait(t, odd, "r+", "r-")
        return yown[s, :, :n] + rq[t, :, :n].astype(F32)

    def gelu(t, total):
        _, _, r0, c0 = item(t)
        value, slope = gelu_parts(total[0])
        ag[0, pl.ds(r0, Q), ycols(c0, 0)] = value.astype(BF16)
        ag[1, pl.ds(r0, Q), ycols(c0, 0)] = (total[1] * slope).astype(BF16)

    def even1(t):
        s = rem(t, SLOTS)
        wait(t, 0, "c")
        y_first(t, 0, lambda dy: mine[s, :, :, ycols(0, dy)] + crecv[t, :, :, ycols(0, dy)].astype(F32))

    def even3(t):
        s = rem(t, SLOTS)
        total = y_last(t, 0)
        zmine[s] = total[:, :Q]
        zs[t, :, :, :CB] = total[:, Q:].astype(BF16)
        start(t, 0, "z")

    def even4(t):
        s = rem(t, SLOTS)
        wait(t, 0, "z")
        gelu(t, zmine[s] + zr[t, :, :, :CB].astype(F32))
        start(t, 0, "Z")

    def even5(t):
        wait(t, 0, "Z")
        start(t, 0, "Y+", "Y-")

    def odd1(t):
        s = rem(t, SLOTS)
        wait(t, 1, "c")
        zs[t] = (mine[s, :, Q:] + crecv[t, :, Q:].astype(F32)).astype(BF16)
        start(t, 1, "z")
        qkeep[s] = mine[s, :, :Q] + crecv[t, :, :Q].astype(F32)

    def odd2(t):
        s = rem(t, SLOTS)
        wait(t, 1, "z")
        y_first(t, 1, lambda dy: qkeep[s, :, :, ycols(0, dy)] + zr[t, :, :, ycols(0, dy)].astype(F32))

    def odd4(t):
        gelu(t, y_last(t, 1))
        start(t, 1, "Y+", "Y-")

    def y_forward(t, odd):
        wait(t, odd, "Y+")
        start(t, odd, "R+")
        wait(t, odd, "Y-")
        start(t, odd, "R-")

    def even7(t):
        wait(t, 0, "R+", "R-")
        start(t, 0, "C")

    def odd6(t):
        wait(t, 1, "R+", "R-")
        start(t, 1, "Z")

    def odd7(t):
        wait(t, 1, "Z")
        start(t, 1, "C")

    def d_copy(i, g, k):
        return remote(dsend.at[i], drecv.at[i], d_send.at[i], d_recv.at[i], dp_peer(g, k))

    def hidden_sum(t):
        g, f, r0, c0 = item(t)
        wait(t, 0, "C")
        part = dot_nt(ag[1, pl.ds(r0, R), pl.ds(c0, FC)], wi[:, pl.ds(c0, FC)])

        @pl.when(f == 0)
        def _():
            acc[pl.ds(r0, R)] = part

        @pl.when(f > 0)
        def _():
            acc[pl.ds(r0, R)] += part

        for gg in range(GROUPS):
            @pl.when(t == gg * NF + NF - 1)
            def _():
                for i, (g2, k) in enumerate(dps):
                    if g2 == gg:
                        rows = pl.multiple_of(g2 * R + slot_of(rem(x + k, NX)) * T, T)
                        dsend[i] = acc[pl.ds(rows, T)].astype(BF16)
                        d_copy(i, g2, k).start()

    factor = 1.0 / math.sqrt(GROUPS * R)

    def weight_grads(t):
        _, _, _, c0 = item(t)
        cols = pl.ds(c0, FC)
        gwi_ref[:, cols] = (dot(xt[...], ag[1, :, cols]) * factor).astype(BF16)
        gwo_ref[cols, :] = (dot_tn(ag[0, :, cols], xg[1]) * factor).astype(BF16)

    both = [
        (even7, odd7), (lambda t: y_forward(t, 0), odd6), (even5, lambda t: y_forward(t, 1)), (even4, odd4),
        (even3, lambda t: y_relay(t, 1)), (lambda t: y_relay(t, 0), odd2), (even1, odd1),
    ]

    @pl.loop(0, ITEMS + LAGS[9])
    def _(tick):
        def at(lag, first, run, other=None):
            t = tick - lag

            @pl.when(jnp.logical_and(t >= first, t < ITEMS))
            def _():
                if other is None:
                    run(t)
                else:
                    lax.cond(is_odd(t), lambda: other(t), lambda: run(t))

        for n, (even, odd) in zip(range(7, 0, -1), both):
            at(LAGS[n], 0, even, odd)
        at(0, 0, products)
        at(LAGS[8], 0, hidden_sum)
        at(LAGS[9], NF, weight_grads)

    total = acc[pl.ds(own, T)]
    for i, (g, k) in enumerate(dps):
        d_copy(i, g, k).wait_recv()
        total = total + drecv[i].astype(F32)
    in_ref[...] = total

    for i, (g, k) in enumerate(dps):
        a_copy(i, g, k)[0].wait_send()
        d_copy(i, g, k).wait_send()

    @pl.loop(0, ITEMS)
    def _(t):
        for odd in range(2):
            @pl.when(is_odd(t) if odd else jnp.logical_not(is_odd(t)))
            def _():
                for name in NAMES:
                    item_copy(t, odd, name)[0].wait_send()


def store_kernel(in_ref, gwi_ref, gwo_ref, in_out, gwi_out, gwo_out, sem):
    copies = [
        pltpu.make_async_copy(gwi_ref, gwi_out, sem.at[0]),
        pltpu.make_async_copy(gwo_ref, gwo_out, sem.at[1]),
        pltpu.make_async_copy(in_ref, in_out, sem.at[2]),
    ]
    for c in copies:
        c.start()
    for c in copies:
        c.wait()


def local(inputs, out_grads, w_in, w_out):
    T, D = inputs.shape
    FF = w_in.shape[1]
    FC = 512
    NF = FF // FC
    R = NX * T
    H, Q, CB = R // 2, R // 4, FC // NY
    ITEMS = GROUPS * NF
    TOK = GROUPS * R
    DPS = GROUPS * NX - 1
    vmem = pl.BlockSpec(memory_space=pltpu.VMEM)
    hbm = pl.BlockSpec(memory_space=pl.ANY)
    dma = pltpu.SemaphoreType.DMA
    shapes = [((T, D), F32), ((D, FF), BF16), ((FF, D), BF16)]
    parts = pl.pallas_call(
        functools.partial(block_kernel, T, D, FC, NF),
        out_shape=[pltpu.VMEM(s, d) for s, d in shapes],
        in_specs=[hbm] * 4,
        out_specs=[vmem] * 3,
        scratch_shapes=[
            pltpu.VMEM((2, TOK, D), BF16),
            pltpu.VMEM((D, TOK), BF16),
            pltpu.VMEM((D, FF), BF16),
            pltpu.VMEM((FF, D), BF16),
            pltpu.VMEM((TOK, D), F32),
            pltpu.VMEM((2, TOK, FF), BF16),
            pltpu.VMEM((ITEMS, 2, H, FC), BF16),
            pltpu.VMEM((ITEMS, 2, H, FC), BF16),
            pltpu.VMEM((SLOTS, 2, H, FC), F32),
            *[pltpu.VMEM((ITEMS, 2, H, CB), BF16)] * 6,
            *[pltpu.VMEM((SLOTS, 2, H, CB), F32)] * 2,
            pltpu.VMEM((SLOTS, 2, Q, CB), F32),
            pltpu.VMEM((SLOTS, 2, Q, FC), F32),
            *[pltpu.VMEM((ITEMS, 2, Q, FC), BF16)] * 2,
            pltpu.VMEM((DPS, T, D), BF16),
            pltpu.VMEM((DPS, T, D), BF16),
            dma((2,)), dma((NF,)), dma((NF,)),
            dma((DPS,)), dma((DPS,)),
            dma((ITEMS, len(NAMES))), dma((ITEMS, len(NAMES))),
            dma((DPS,)), dma((DPS,)),
        ],
        compiler_params=pltpu.CompilerParams(
            collective_id=0, has_side_effects=True, vmem_limit_bytes=44 * 2**20
        ),
        name="ffn_backward",
    )(inputs, out_grads, w_in, w_out)
    return pl.pallas_call(
        store_kernel,
        out_shape=[jax.ShapeDtypeStruct(s, d) for s, d in shapes],
        in_specs=[vmem] * 3,
        out_specs=[hbm] * 3,
        scratch_shapes=[dma((3,))],
        compiler_params=pltpu.CompilerParams(vmem_limit_bytes=2**20),
        name="store_results",
    )(*parts)


def solution(mesh):
    return jax.shard_map(
        local,
        mesh=mesh,
        in_specs=(P("dp", "mp"), P("dp", "mp"), P("mp", "dp"), P("dp", "mp")),
        out_specs=(P("dp", "mp"), P("mp", "dp"), P("dp", "mp")),
        check_vma=False,
    )
```

```python
import functools
import math

import jax
import jax.numpy as jnp
from jax import lax
from jax.experimental import pallas as pl
from jax.experimental.pallas import tpu as pltpu
from jax.sharding import PartitionSpec as P

MESH = pl.DeviceIdType.MESH
F32, BF16 = jnp.float32, jnp.bfloat16

NX, NY = 4, 4
FACTOR = 1.0 / math.sqrt(256)
GROUPS = 2
COLS = 512
ITEMS = (
    (0, 0, 3, 1),
    (0, 3, 3, 0),
    (0, 6, 3, 0),
    (1, 0, 2, 1),
    (1, 2, 3, 0),
    (1, 5, 2, 1),
    (1, 7, 2, 0),
)
ORDER = (
    (0, 0), (1, 0), (0, 1), (2, 0), (1, 1), (3, 0), (2, 1), (4, 0), (3, 1), (1, 2),
    (0, 2), (5, 0), (4, 1), (2, 2), (6, 0), (5, 1), (3, 2), (1, 3), (0, 3), (6, 1),
    (4, 2), (2, 3), (3, 3), (0, 4), (0, 9), (5, 2), (6, 2), (1, 4), (1, 9), (4, 3),
    (2, 4), (3, 4), (0, 5), (3, 9), (2, 9), (0, 10), (5, 3), (1, 5), (1, 10), (6, 3),
    (3, 5), (0, 6), (4, 4), (4, 9), (3, 10), (2, 5), (0, 11), (5, 4), (5, 9), (2, 10),
    (6, 4), (1, 6), (6, 9), (1, 11), (3, 6), (3, 11), (0, 7), (2, 6), (4, 5), (5, 5),
    (4, 10), (5, 10), (0, 8), (2, 11), (1, 7), (0, 12), (1, 12), (6, 5), (2, 7), (6, 10),
    (1, 8), (5, 6), (4, 6), (1, 13), (0, 13), (3, 7), (2, 8), (5, 11), (4, 11), (3, 8),
    (3, 12), (2, 12), (6, 6), (3, 14), (6, 11), (5, 7), (4, 7), (3, 13), (2, 13), (3, 15),
    (6, 7), (5, 8), (4, 8), (6, 12), (5, 12), (6, 8), (4, 12), (4, 14), (6, 13), (5, 13),
    (5, 14), (4, 13), (6, 14), (4, 15),
)
STORED_LATE = 4
SUMS = ("c", "y+", "y-", "r+", "r-", "z")
GATHERS = tuple((name, a) for a in range(2) for name in ("Z", "Y+", "Y-", "R+", "R-", "C"))
NAMES = SUMS + GATHERS


def rem(a, b):
    return lax.rem(a, jnp.int32(b))


def div(a, b):
    return lax.div(a, jnp.int32(b))


def mult(v, m):
    return pl.multiple_of(v * m, m)


def dot(a, b):
    return lax.dot_general(a, b, (((1,), (0,)), ((), ())), preferred_element_type=F32)


def dot_nt(a, b):
    return lax.dot_general(a, b, (((1,), (1,)), ((), ())), preferred_element_type=F32)


def dot_tn(a, b):
    return lax.dot_general(a, b, (((0,), (0,)), ((), ())), preferred_element_type=F32)


def gelu_parts(v):
    cumul = 0.5 * (1.0 + lax.erf(v * (1.0 / math.sqrt(2.0))))
    density = jnp.exp(-0.5 * v * v) * (1.0 / math.sqrt(2.0 * math.pi))
    return v * cumul, cumul + v * density


def block_kernel(
    T, D, NF,
    x_hbm, g_hbm, wi_hbm, wo_hbm,
    in_ref, gwi_ref, gwo_ref, xg, ag,
    xt, wi, wo, acc,
    csend, crecv, mine, yp, ym, yq, rp, rm, rq, yown, yrel, zmine, zs, zr, zsw, zrw, dsend, drecv,
    load_sem, wi_sem, wo_sem, a_send, a_recv, i_send, i_recv, d_send, d_recv,
):
    R = NX * T
    H, Q = R // 2, R // 4
    dp, mp = lax.axis_index("dp"), lax.axis_index("mp")
    x, zhi = div(dp, 2), rem(dp, 2)
    zlo, y, core = div(mp, 8), rem(div(mp, 2), NY), rem(mp, 2)

    def slot_of(j):
        return rem(div(j, 2) + core, 2) * 2 + rem(rem(j, 2) + zlo, 2)

    def mp_peer(dz=0, dy=0, dc=0):
        return (dp, rem(zlo + dz, 2) * 8 + rem(y + dy, NY) * 2 + rem(core + dc, 2))

    def dp_peer(g, k):
        return (rem(x + k, NX) * 2 + rem(zhi + g, 2), mp)

    peers = [mp_peer(dc=1), mp_peer(dz=1)] + [mp_peer(dy=k) for k in range(1, NY)]
    dps = [(g, k) for g in range(GROUPS) for k in range(NX) if g or k]
    barrier = pltpu.get_barrier_semaphore()
    for peer in peers + [dp_peer(g, k) for g, k in dps]:
        pl.semaphore_signal(barrier, inc=1, device_id=peer, device_id_type=MESH)

    own = mult(slot_of(x), T)
    loads = [
        pltpu.make_async_copy(x_hbm, xg.at[0, pl.ds(own, T)], load_sem.at[0]),
        pltpu.make_async_copy(g_hbm, xg.at[1, pl.ds(own, T)], load_sem.at[1]),
    ]
    for c in loads:
        c.start()

    def wi_copy(f):
        cols = pl.ds(f * COLS, COLS)
        return pltpu.make_async_copy(wi_hbm.at[:, cols], wi.at[:, cols], wi_sem.at[f])

    def wo_copy(f):
        rows = pl.ds(f * COLS, COLS)
        return pltpu.make_async_copy(wo_hbm.at[rows], wo.at[rows], wo_sem.at[f])

    for f in range(NF):
        wi_copy(f).start()
        wo_copy(f).start()

    def remote(src, dst, send, recv, peer):
        return pltpu.make_async_remote_copy(
            src_ref=src, dst_ref=dst, send_sem=send, recv_sem=recv, device_id=peer, device_id_type=MESH
        )

    def a_copy(i, g, k):
        src = xg.at[:, pl.ds(pl.multiple_of((R if k and g else 0) + own, T), T)]
        dst = xg.at[:, pl.ds(pl.multiple_of(g * R + own, T), T)]
        land = xg.at[:, pl.ds(pl.multiple_of(g * R + slot_of(rem(x + NX - k, NX)) * T, T), T)]
        peer = dp_peer(0, k) if k else dp_peer(g, 0)
        return remote(src, dst, a_send.at[i], a_recv.at[i], peer), remote(land, land, a_send.at[i], a_recv.at[i], peer)

    def gather_start(pick):
        for i, (g, k) in enumerate(dps):
            if pick(g, k):
                a_copy(i, g, k)[0].start()

    def gather_wait(pick):
        for i, (g, k) in enumerate(dps):
            if pick(g, k):
                a_copy(i, g, k)[1].wait_recv()

    for c in loads:
        c.wait()
    pl.semaphore_wait(barrier, len(peers) + len(dps))
    gather_start(lambda g, k: g == 0)
    gather_start(lambda g, k: k == 0)

    class Item:
        def __init__(self, i):
            g, f, n, self.odd = ITEMS[i]
            self.i, self.g, self.f, self.n = i, g, f, n
            self.r0, self.c0, self.width = g * R, f * COLS, n * COLS
            self.block = self.width // NY
            self.cols = pl.ds(self.c0, self.width)
            self.bcols = pl.ds(self.c0 // NY, self.block)
            self.rows = Q if self.odd else H

        def ycols(self, dy):
            start = self.c0 + rem(y + dy, NY) * self.block
            return pl.ds(pl.multiple_of(start, 128), self.block)

    def item_copy(it, name):
        g, r0, bc, n = it.g, it.r0, it.bcols, NAMES.index(name)
        up, down, zp, cp = mp_peer(dy=1), mp_peer(dy=NY - 1), mp_peer(dz=1), mp_peer(dc=1)
        head, own_z, other_z, gather = pl.ds(0, it.rows), pl.ds(r0, Q), pl.ds(r0 + Q, Q), pl.ds(r0, it.rows)
        land = None
        if name == "c":
            src, dst, peer = csend.at[g, :, :, it.cols], crecv.at[g, :, :, it.cols], cp
        elif name == "y+":
            src, dst, peer = yp.at[g, :, head, bc], rp.at[g, :, head, bc], up
        elif name == "y-":
            src, dst, peer = ym.at[g, :, head, bc], rm.at[g, :, head, bc], down
        elif name == "r+":
            src, dst, peer = yq.at[g, 0, head, bc], rq.at[g, 0, head, bc], up
        elif name == "r-":
            src, dst, peer = yq.at[g, 1, head, bc], rq.at[g, 1, head, bc], down
        elif name == "z" and it.odd:
            src, dst, peer = zsw.at[g, :, :, it.cols], zrw.at[g, :, :, it.cols], zp
        elif name == "z":
            src, dst, peer = zs.at[g, :, :, bc], zr.at[g, :, :, bc], zp
        else:
            name, a = name
            half = it.rows // 2
            if name == "Z":
                zc = it.cols if it.odd else it.ycols(0)
                src, dst, peer = ag.at[a, own_z, zc], ag.at[a, other_z, zc], zp
            elif name == "Y+":
                src = dst = ag.at[a, gather, it.ycols(0)]
                land, peer = ag.at[a, gather, it.ycols(NY - 1)], up
            elif name == "Y-":
                src = dst = ag.at[a, gather, it.ycols(0)]
                land, peer = ag.at[a, gather, it.ycols(1)], down
            elif name == "R+":
                src = dst = ag.at[a, pl.ds(r0, half), it.ycols(NY - 1)]
                land, peer = ag.at[a, pl.ds(r0, half), it.ycols(2)], up
            elif name == "R-":
                src = dst = ag.at[a, pl.ds(r0 + half, half), it.ycols(1)]
                land, peer = ag.at[a, pl.ds(r0 + half, half), it.ycols(2)], down
            else:
                src, dst, peer = ag.at[a, pl.ds(r0, H), it.cols], ag.at[a, pl.ds(r0 + H, H), it.cols], cp
        land = dst if land is None else land
        send, recv = i_send.at[it.i, n], i_recv.at[it.i, n]
        return src, dst, land, send, recv, peer

    def start(it, *names):
        for name in names:
            src, dst, _, send, recv, peer = item_copy(it, name)
            remote(src, dst, send, recv, peer).start()

    def wait(it, *names):
        for name in names:
            _, _, land, send, recv, peer = item_copy(it, name)
            remote(land, land, send, recv, peer).wait_recv()

    def products(it):
        if it.i == 0:
            gather_wait(lambda g, k: g == 0)
        if it.i == 1:
            gather_wait(lambda g, k: k == 0)
            gather_start(lambda g, k: g and k)
        if it.g == 1 and it.f == 0:
            gather_wait(lambda g, k: g and k)
            xt[...] = xg[0].T
        if it.g == 0:
            for f in range(it.f, it.f + it.n):
                wi_copy(f).wait()
                wo_copy(f).wait()

        def chunk(c0):
            cols = pl.ds(c0, COLS)
            pre = dot(xg[0, pl.ds(it.r0, R)], wi[:, cols])
            mine[it.g, 0, :, cols] = pre[:H]
            csend[it.g, 0, :, cols] = pre[H:].astype(BF16)
            grad = dot_nt(xg[1, pl.ds(it.r0, R)], wo[cols])
            mine[it.g, 1, :, cols] = grad[:H]
            csend[it.g, 1, :, cols] = grad[H:].astype(BF16)

        chunks(it, chunk)
        start(it, "c")

    def chunks(it, run):
        if it.n == 1:
            run(it.c0)
        else:
            @pl.loop(0, it.n)
            def _(j):
                run(pl.multiple_of(it.c0 + j * COLS, COLS))

    def y_first(it, block):
        g, h, bc = it.g, pl.ds(0, it.rows), it.bcols
        b = block(2)
        yp[g, 0, h, bc] = b[0].astype(BF16)
        ym[g, 1, h, bc] = b[1].astype(BF16)
        b = block(1)
        yrel[g, 0, h, bc] = b[0]
        yp[g, 1, h, bc] = b[1].astype(BF16)
        start(it, "y+")
        b = block(3)
        yrel[g, 1, h, bc] = b[1]
        ym[g, 0, h, bc] = b[0].astype(BF16)
        start(it, "y-")
        yown[g, :, h, bc] = block(0)

    def y_relay(it):
        g, h, bc = it.g, pl.ds(0, it.rows), it.bcols
        wait(it, "y+")
        yq[g, 0, h, bc] = (yrel[g, 0, h, bc] + rp[g, 0, h, bc].astype(F32)).astype(BF16)
        start(it, "r+")
        wait(it, "y-")
        yq[g, 1, h, bc] = (yrel[g, 1, h, bc] + rm[g, 1, h, bc].astype(F32)).astype(BF16)
        start(it, "r-")
        yown[g, 0, h, bc] += rm[g, 0, h, bc].astype(F32)
        yown[g, 1, h, bc] += rp[g, 1, h, bc].astype(F32)

    def y_last(it):
        g, h, bc = it.g, pl.ds(0, it.rows), it.bcols
        wait(it, "r+", "r-")
        return yown[g, :, h, bc] + rq[g, :, h, bc].astype(F32)

    def gelu(it, total):
        value, slope = gelu_parts(total[0])
        ag[0, pl.ds(it.r0, Q), it.ycols(0)] = value.astype(BF16)
        ag[1, pl.ds(it.r0, Q), it.ycols(0)] = (total[1] * slope).astype(BF16)

    def even1(it):
        wait(it, "c")
        y_first(it, lambda dy: mine[it.g, :, :, it.ycols(dy)] + crecv[it.g, :, :, it.ycols(dy)].astype(F32))

    def even3(it):
        total = y_last(it)
        zs[it.g, :, :, it.bcols] = total[:, Q:].astype(BF16)
        start(it, "z")
        zmine[it.g, :, :, it.bcols] = total[:, :Q]

    def even4(it):
        wait(it, "z")
        gelu(it, zmine[it.g, :, :, it.bcols] + zr[it.g, :, :, it.bcols].astype(F32))
        start(it, ("Z", 1))

    def even9(it):
        start(it, ("Z", 0))

    def y_gather(it, a):
        wait(it, ("Z", a))
        start(it, ("Y+", a), ("Y-", a))

    def odd1(it):
        g, low, high, c = it.g, pl.ds(0, Q), pl.ds(Q, Q), it.cols
        wait(it, "c")
        zsw[g, :, :, c] = (mine[g, :, high, c] + crecv[g, :, high, c].astype(F32)).astype(BF16)
        start(it, "z")
        mine[g, :, low, c] += crecv[g, :, low, c].astype(F32)

    def odd2(it):
        wait(it, "z")
        y_first(it, lambda dy: mine[it.g, :, pl.ds(0, Q), it.ycols(dy)] + zrw[it.g, :, :, it.ycols(dy)].astype(F32))

    def odd4(it):
        gelu(it, y_last(it))
        start(it, ("Y+", 1), ("Y-", 1))

    def odd9(it):
        start(it, ("Y+", 0), ("Y-", 0))

    def y_forward(it, a):
        wait(it, ("Y+", a))
        start(it, ("R+", a))
        wait(it, ("Y-", a))
        start(it, ("R-", a))

    def even_core(it, a):
        wait(it, ("R+", a), ("R-", a))
        start(it, ("C", a))

    def z_gather(it, a):
        wait(it, ("R+", a), ("R-", a))
        start(it, ("Z", a))

    def odd_core(it, a):
        wait(it, ("Z", a))
        start(it, ("C", a))

    def end(it):
        wait(it, ("C", 0))

    def d_copy(i, g, k):
        return remote(dsend.at[i], drecv.at[i], d_send.at[i], d_recv.at[i], dp_peer(g, k))

    summed = [0] * GROUPS

    def hidden_sum(it):
        wait(it, ("C", 1))

        def chunk(c0):
            cols = pl.ds(c0, COLS)
            acc[pl.ds(it.r0, R)] += dot_nt(ag[1, pl.ds(it.r0, R), cols], wi[:, cols])

        chunks(it, chunk)
        summed[it.g] += it.n
        if summed[it.g] == NF:
            for i, (g, k) in enumerate(dps):
                if g == it.g:
                    rows = pl.multiple_of(g * R + slot_of(rem(x + k, NX)) * T, T)
                    dsend[i] = acc[pl.ds(rows, T)].astype(BF16)
                    d_copy(i, g, k).start()

    def grad_w_in(it):
        def chunk(c0):
            cols = pl.ds(c0, COLS)
            gwi_ref[:, cols] = (dot(xt[...], ag[1, :, cols]) * FACTOR).astype(BF16)

        chunks(it, chunk)

    def grad_w_out(it):
        def chunk(c0):
            cols = pl.ds(c0, COLS)
            gwo_ref[cols, :] = (dot_tn(ag[0, :, cols], xg[1]) * FACTOR).astype(BF16)

        chunks(it, chunk)

    acc[...] = jnp.zeros_like(acc)

    def of(stage, a):
        return lambda it: stage(it, a)

    tail = (end, grad_w_in, grad_w_out)
    stages = (
        (products, even1, y_relay, even3, even4, of(y_gather, 1), of(y_forward, 1), of(even_core, 1), hidden_sum)
        + (even9, of(y_gather, 0), of(y_forward, 0), of(even_core, 0)) + tail,
        (products, odd1, odd2, y_relay, odd4, of(y_forward, 1), of(z_gather, 1), of(odd_core, 1), hidden_sum)
        + (odd9, of(y_forward, 0), of(z_gather, 0), of(odd_core, 0)) + tail,
    )
    items = [Item(i) for i in range(len(ITEMS))]
    for i, n in ORDER:
        stages[items[i].odd][n](items[i])

    total = acc[pl.ds(own, T)]
    for i, (g, k) in enumerate(dps):
        d_copy(i, g, k).wait_recv()
        total = total + drecv[i].astype(F32)
    in_ref[...] = total

    for i, (g, k) in enumerate(dps):
        a_copy(i, g, k)[0].wait_send()
        d_copy(i, g, k).wait_send()
    for it in items:
        for name in NAMES:
            src, dst, _, send, recv, peer = item_copy(it, name)
            remote(src, dst, send, recv, peer).wait_send()


def store_kernel(done, in_ref, gwi_ref, gwo_ref, xg, ag, in_out, gwi_out, gwo_out, gwo, sem):
    head = pl.ds(0, done)
    copies = [
        pltpu.make_async_copy(gwo_ref, gwo_out.at[head], sem.at[2]),
        pltpu.make_async_copy(gwi_ref, gwi_out, sem.at[1]),
        pltpu.make_async_copy(in_ref, in_out, sem.at[0]),
    ]
    for c in copies:
        c.start()
    for i, c0 in enumerate(range(done, ag.shape[2], COLS)):
        cols = pl.ds(c0, COLS)
        gwo[i] = (dot_tn(ag[0, :, cols], xg[1]) * FACTOR).astype(BF16)
        copies.append(pltpu.make_async_copy(gwo.at[i], gwo_out.at[cols], sem.at[3 + i]))
        copies[-1].start()
    for c in copies:
        c.wait()


def local(inputs, out_grads, w_in, w_out):
    T, D = inputs.shape
    FF = w_in.shape[1]
    NF = FF // COLS
    R = NX * T
    H, Q, TOK, BF = R // 2, R // 4, GROUPS * R, FF // NY
    DPS = GROUPS * NX - 1
    done = FF - STORED_LATE * COLS
    vmem = pl.BlockSpec(memory_space=pltpu.VMEM)
    hbm = pl.BlockSpec(memory_space=pl.ANY)
    dma = pltpu.SemaphoreType.DMA
    G = GROUPS
    parts = pl.pallas_call(
        functools.partial(block_kernel, T, D, NF),
        out_shape=[
            pltpu.VMEM((T, D), F32),
            pltpu.VMEM((D, FF), BF16),
            pltpu.VMEM((done, D), BF16),
            pltpu.VMEM((2, TOK, D), BF16),
            pltpu.VMEM((2, TOK, FF), BF16),
        ],
        in_specs=[hbm] * 4,
        out_specs=[vmem] * 5,
        scratch_shapes=[
            pltpu.VMEM((D, TOK), BF16),
            pltpu.VMEM((D, FF), BF16),
            pltpu.VMEM((FF, D), BF16),
            pltpu.VMEM((TOK, D), F32),
            pltpu.VMEM((G, 2, H, FF), BF16),
            pltpu.VMEM((G, 2, H, FF), BF16),
            pltpu.VMEM((G, 2, H, FF), F32),
            *[pltpu.VMEM((G, 2, H, BF), BF16)] * 6,
            *[pltpu.VMEM((G, 2, H, BF), F32)] * 2,
            pltpu.VMEM((G, 2, Q, BF), F32),
            *[pltpu.VMEM((G, 2, Q, BF), BF16)] * 2,
            *[pltpu.VMEM((G, 2, Q, FF), BF16)] * 2,
            pltpu.VMEM((DPS, T, D), BF16),
            pltpu.VMEM((DPS, T, D), BF16),
            dma((2,)), dma((NF,)), dma((NF,)),
            dma((DPS,)), dma((DPS,)),
            dma((len(ITEMS), len(NAMES))), dma((len(ITEMS), len(NAMES))),
            dma((DPS,)), dma((DPS,)),
        ],
        compiler_params=pltpu.CompilerParams(
            collective_id=0, has_side_effects=True, vmem_limit_bytes=38 * 2**20
        ),
        name="ffn_backward",
    )(inputs, out_grads, w_in, w_out)
    return pl.pallas_call(
        functools.partial(store_kernel, done),
        out_shape=[
            jax.ShapeDtypeStruct((T, D), F32),
            jax.ShapeDtypeStruct((D, FF), BF16),
            jax.ShapeDtypeStruct((FF, D), BF16),
        ],
        in_specs=[vmem] * 5,
        out_specs=[hbm] * 3,
        scratch_shapes=[
            pltpu.VMEM((max(STORED_LATE, 1), COLS, D), BF16),
            dma((3 + STORED_LATE,)),
        ],
        compiler_params=pltpu.CompilerParams(vmem_limit_bytes=12 * 2**20),
        name="store_results",
    )(*parts)


def solution(mesh):
    return jax.shard_map(
        local,
        mesh=mesh,
        in_specs=(P("dp", "mp"), P("dp", "mp"), P("mp", "dp"), P("dp", "mp")),
        out_specs=(P("dp", "mp"), P("mp", "dp"), P("dp", "mp")),
        check_vma=False,
    )
```

```python
import functools
import math

import jax
import jax.numpy as jnp
from jax import lax
from jax.experimental import pallas as pl
from jax.experimental.pallas import tpu as pltpu
from jax.sharding import PartitionSpec as P

MESH = pl.DeviceIdType.MESH
F32, BF16 = jnp.float32, jnp.bfloat16

NX, NY = 4, 4
FACTOR = 1.0 / math.sqrt(256)
PLACES = (((0, 0), (1, 0), (3, 0), (0, 1)), ((2, 0), (1, 1), (3, 1), (2, 1)))
GROUPS = len(PLACES)
COLS = 512
ITEMS = (
    (0, 0, 2, 1),
    (0, 2, 3, 0),
    (0, 5, 2, 1),
    (0, 7, 2, 0),
    (1, 0, 2, 1),
    (1, 2, 2, 1),
    (1, 4, 2, 0),
    (1, 6, 2, 0),
    (1, 8, 1, 1),
)
ORDER = (
    (0, 0), (1, 0), (0, 1), (2, 0), (1, 1), (3, 0), (2, 1), (4, 0), (3, 1), (0, 2),
    (5, 0), (4, 1), (1, 2), (6, 0), (5, 1), (3, 2), (2, 2), (0, 3), (7, 0), (6, 1),
    (1, 3), (8, 0), (4, 2), (7, 1), (3, 3), (2, 3), (0, 4), (8, 1), (5, 2), (6, 2),
    (1, 4), (4, 3), (3, 4), (0, 9), (7, 2), (2, 4), (8, 2), (0, 5), (5, 3), (1, 5),
    (6, 3), (3, 5), (4, 4), (1, 9), (0, 10), (7, 3), (2, 5), (8, 3), (0, 6), (5, 4),
    (2, 9), (6, 4), (3, 9), (1, 10), (1, 6), (3, 6), (7, 4), (4, 5), (4, 9), (2, 6),
    (8, 4), (8, 9), (5, 5), (7, 9), (6, 9), (0, 7), (5, 9), (2, 10), (6, 5), (0, 11),
    (3, 10), (1, 11), (7, 5), (1, 7), (0, 8), (4, 6), (3, 7), (4, 10), (8, 5), (8, 10),
    (2, 7), (5, 6), (7, 10), (5, 10), (2, 11), (6, 10), (1, 8), (6, 6), (2, 8), (3, 11),
    (0, 12), (1, 12), (3, 8), (7, 6), (8, 6), (4, 7), (8, 11), (4, 11), (0, 13), (7, 11),
    (1, 13), (5, 11), (5, 7), (6, 11), (4, 8), (6, 7), (3, 12), (4, 14), (7, 7), (2, 12),
    (8, 7), (7, 12), (5, 8), (8, 12), (3, 13), (6, 12), (6, 8), (7, 8), (2, 13), (8, 8),
    (8, 13), (7, 13), (6, 13), (4, 12), (5, 14), (5, 12), (6, 14), (4, 13), (7, 14), (5, 13),
    (8, 14), (4, 15), (5, 15), (6, 15),
)
STORED_LATE = 3
SUMS = ("y+", "y-", "r+", "r-", "z")
GATHERS = tuple((name, a) for a in range(2) for name in ("Z", "Y+", "Y-", "R+", "R-", "C"))
NAMES = SUMS + GATHERS


def rem(a, b):
    return lax.rem(a, jnp.int32(b))


def div(a, b):
    return lax.div(a, jnp.int32(b))


def dot(a, b):
    return lax.dot_general(a, b, (((1,), (0,)), ((), ())), preferred_element_type=F32)


def dot_nt(a, b):
    return lax.dot_general(a, b, (((1,), (1,)), ((), ())), preferred_element_type=F32)


def dot_tn(a, b):
    return lax.dot_general(a, b, (((0,), (0,)), ((), ())), preferred_element_type=F32)


def gelu_parts(v):
    cumul = 0.5 * (1.0 + lax.erf(v * (1.0 / math.sqrt(2.0))))
    density = jnp.exp(-0.5 * v * v) * (1.0 / math.sqrt(2.0 * math.pi))
    return v * cumul, cumul + v * density


def block_kernel(
    T, D, NF,
    x_hbm, g_hbm, wi_hbm, wo_hbm,
    in_ref, gwi_ref, gwo_ref, xg, ag,
    xt, wi, wo, acc,
    csend, crecv, mine, yp, ym, yq, rp, rm, rq, yown, yrel, zmine, zs, zr, zsw, zrw, dsend, drecv,
    load_sem, wi_sem, wo_sem, a_send, a_recv, c_send, c_recv, i_send, i_recv, d_send, d_recv,
):
    R = NX * T
    H, Q = R // 2, R // 4
    dp, mp = lax.axis_index("dp"), lax.axis_index("mp")
    x, zhi = div(dp, 2), rem(dp, 2)
    zlo, y, core = div(mp, 8), rem(div(mp, 2), NY), rem(mp, 2)

    def rows_of(g, j):
        slot = rem(j // 2 + core, 2) * 2 + rem(j % 2 + zlo, 2)
        return pl.ds(pl.multiple_of(g * R + slot * T, T), T)

    def rows_from(dx, dz):
        for g, places in enumerate(PLACES):
            if (dx, dz) in places:
                return rows_of(g, places.index((dx, dz)))

    def mp_peer(dz=0, dy=0, dc=0):
        return (dp, rem(zlo + dz, 2) * 8 + rem(y + dy, NY) * 2 + rem(core + dc, 2))

    def dp_peer(dx, dz):
        return (rem(x + dx, NX) * 2 + rem(zhi + dz, 2), mp)

    peers = [mp_peer(dc=1), mp_peer(dz=1)] + [mp_peer(dy=k) for k in range(1, NY)]
    dps = [place for places in PLACES for place in places if place != (0, 0)]
    barrier = pltpu.get_barrier_semaphore()
    for peer in peers + [dp_peer(*place) for place in dps]:
        pl.semaphore_signal(barrier, inc=1, device_id=peer, device_id_type=MESH)

    own = rows_of(0, 0)
    loads = [
        pltpu.make_async_copy(x_hbm, xg.at[0, own], load_sem.at[0]),
        pltpu.make_async_copy(g_hbm, xg.at[1, own], load_sem.at[1]),
    ]
    for c in loads:
        c.start()

    def wi_copy(f):
        cols = pl.ds(f * COLS, COLS)
        return pltpu.make_async_copy(wi_hbm.at[:, cols], wi.at[:, cols], wi_sem.at[f])

    def wo_copy(f):
        rows = pl.ds(f * COLS, COLS)
        return pltpu.make_async_copy(wo_hbm.at[rows], wo.at[rows], wo_sem.at[f])

    for f in range(NF):
        wi_copy(f).start()
        wo_copy(f).start()

    def remote(src, dst, send, recv, peer):
        return pltpu.make_async_remote_copy(
            src_ref=src, dst_ref=dst, send_sem=send, recv_sem=recv, device_id=peer, device_id_type=MESH
        )

    def a_copy(i):
        dx, dz = dps[i]
        back = (-dx) % NX
        src = rows_from(0, 1) if dx and dz else own
        peer = dp_peer(dx, 0) if dx else dp_peer(0, dz)
        rows = rows_from(back, dz)
        send = remote(xg.at[:, src], xg.at[:, rows], a_send.at[i], a_recv.at[i], peer)
        return send, remote(xg.at[:, rows], xg.at[:, rows], a_send.at[i], a_recv.at[i], peer)

    def gather_start(*places):
        for place in places:
            a_copy(dps.index(place))[0].start()

    def gather_wait(*places):
        for place in places:
            a_copy(dps.index(place))[1].wait_recv()

    near, partner = ((1, 0), (3, 0)), (0, 1)
    opposite, beyond = (2, 0), ((1, 1), (3, 1), (2, 1))

    for c in loads:
        c.wait()
    pl.semaphore_wait(barrier, len(peers) + len(dps))
    gather_start(*near, partner)

    class Item:
        def __init__(self, i):
            g, f, n, self.odd = ITEMS[i]
            self.i, self.g, self.f, self.n = i, g, f, n
            self.r0, self.c0, self.width = g * R, f * COLS, n * COLS
            self.block = self.width // NY
            self.cols = pl.ds(self.c0, self.width)
            self.bcols = pl.ds(self.c0 // NY, self.block)
            self.rows = Q if self.odd else H

        def ycols(self, dy):
            start = self.c0 + rem(y + dy, NY) * self.block
            return pl.ds(pl.multiple_of(start, 128), self.block)

    def item_copy(it, name):
        g, r0, bc, n = it.g, it.r0, it.bcols, NAMES.index(name)
        up, down, zp, cp = mp_peer(dy=1), mp_peer(dy=NY - 1), mp_peer(dz=1), mp_peer(dc=1)
        head, own_z, other_z, gather = pl.ds(0, it.rows), pl.ds(r0, Q), pl.ds(r0 + Q, Q), pl.ds(r0, it.rows)
        land = None
        if name == "y+":
            src, dst, peer = yp.at[g, :, head, bc], rp.at[g, :, head, bc], up
        elif name == "y-":
            src, dst, peer = ym.at[g, :, head, bc], rm.at[g, :, head, bc], down
        elif name == "r+":
            src, dst, peer = yq.at[g, 0, head, bc], rq.at[g, 0, head, bc], up
        elif name == "r-":
            src, dst, peer = yq.at[g, 1, head, bc], rq.at[g, 1, head, bc], down
        elif name == "z" and it.odd:
            src, dst, peer = zsw.at[g, :, :, it.cols], zrw.at[g, :, :, it.cols], zp
        elif name == "z":
            src, dst, peer = zs.at[g, :, :, bc], zr.at[g, :, :, bc], zp
        else:
            name, a = name
            half = it.rows // 2
            if name == "Z":
                zc = it.cols if it.odd else it.ycols(0)
                src, dst, peer = ag.at[a, own_z, zc], ag.at[a, other_z, zc], zp
            elif name == "Y+":
                src = dst = ag.at[a, gather, it.ycols(0)]
                land, peer = ag.at[a, gather, it.ycols(NY - 1)], up
            elif name == "Y-":
                src = dst = ag.at[a, gather, it.ycols(0)]
                land, peer = ag.at[a, gather, it.ycols(1)], down
            elif name == "R+":
                src = dst = ag.at[a, pl.ds(r0, half), it.ycols(NY - 1)]
                land, peer = ag.at[a, pl.ds(r0, half), it.ycols(2)], up
            elif name == "R-":
                src = dst = ag.at[a, pl.ds(r0 + half, half), it.ycols(1)]
                land, peer = ag.at[a, pl.ds(r0 + half, half), it.ycols(2)], down
            else:
                src, dst, peer = ag.at[a, pl.ds(r0, H), it.cols], ag.at[a, pl.ds(r0 + H, H), it.cols], cp
        land = dst if land is None else land
        send, recv = i_send.at[it.i, n], i_recv.at[it.i, n]
        return src, dst, land, send, recv, peer

    def start(it, *names):
        for name in names:
            src, dst, _, send, recv, peer = item_copy(it, name)
            remote(src, dst, send, recv, peer).start()

    def wait(it, *names):
        for name in names:
            _, _, land, send, recv, peer = item_copy(it, name)
            remote(land, land, send, recv, peer).wait_recv()

    def core_copy(g, c0):
        cols, n = pl.ds(c0, COLS), g * NF + c0 // COLS
        return remote(csend.at[g, :, :, cols], crecv.at[g, :, :, cols], c_send.at[n], c_recv.at[n], mp_peer(dc=1))

    def core_wait(it):
        for f in range(it.f, it.f + it.n):
            core_copy(it.g, f * COLS).wait_recv()

    def products(it):
        if it.i == 0:
            gather_wait(*near, partner)
            gather_start(opposite, *beyond)
        if it.g == 1 and it.f == 0:
            gather_wait(opposite, *beyond)
            xt[...] = xg[0].T
        if it.g == 0:
            for f in range(it.f, it.f + it.n):
                wi_copy(f).wait()
                wo_copy(f).wait()

        def chunk(c0):
            cols = pl.ds(c0, COLS)
            pre = dot(xg[0, pl.ds(it.r0, R)], wi[:, cols])
            mine[it.g, 0, :, cols] = pre[:H]
            csend[it.g, 0, :, cols] = pre[H:].astype(BF16)
            grad = dot_nt(xg[1, pl.ds(it.r0, R)], wo[cols])
            mine[it.g, 1, :, cols] = grad[:H]
            csend[it.g, 1, :, cols] = grad[H:].astype(BF16)
            core_copy(it.g, c0).start()

        chunks(it, chunk)

    def chunks(it, run):
        if it.n == 1:
            run(it.c0)
        else:
            @pl.loop(0, it.n)
            def _(j):
                run(pl.multiple_of(it.c0 + j * COLS, COLS))

    def y_first(it, block):
        g, h, bc = it.g, pl.ds(0, it.rows), it.bcols
        b = block(2)
        yp[g, 0, h, bc] = b[0].astype(BF16)
        ym[g, 1, h, bc] = b[1].astype(BF16)
        b = block(1)
        yrel[g, 0, h, bc] = b[0]
        yp[g, 1, h, bc] = b[1].astype(BF16)
        start(it, "y+")
        b = block(3)
        yrel[g, 1, h, bc] = b[1]
        ym[g, 0, h, bc] = b[0].astype(BF16)
        start(it, "y-")
        yown[g, :, h, bc] = block(0)

    def y_relay(it):
        g, h, bc = it.g, pl.ds(0, it.rows), it.bcols
        wait(it, "y+")
        yq[g, 0, h, bc] = (yrel[g, 0, h, bc] + rp[g, 0, h, bc].astype(F32)).astype(BF16)
        start(it, "r+")
        wait(it, "y-")
        yq[g, 1, h, bc] = (yrel[g, 1, h, bc] + rm[g, 1, h, bc].astype(F32)).astype(BF16)
        start(it, "r-")
        yown[g, 0, h, bc] += rm[g, 0, h, bc].astype(F32)
        yown[g, 1, h, bc] += rp[g, 1, h, bc].astype(F32)

    def y_last(it):
        g, h, bc = it.g, pl.ds(0, it.rows), it.bcols
        wait(it, "r+", "r-")
        return yown[g, :, h, bc] + rq[g, :, h, bc].astype(F32)

    def gelu(it, total):
        value, slope = gelu_parts(total[0])
        ag[0, pl.ds(it.r0, Q), it.ycols(0)] = value.astype(BF16)
        ag[1, pl.ds(it.r0, Q), it.ycols(0)] = (total[1] * slope).astype(BF16)

    def even1(it):
        core_wait(it)
        y_first(it, lambda dy: mine[it.g, :, :, it.ycols(dy)] + crecv[it.g, :, :, it.ycols(dy)].astype(F32))

    def even3(it):
        total = y_last(it)
        zs[it.g, :, :, it.bcols] = total[:, Q:].astype(BF16)
        start(it, "z")
        zmine[it.g, :, :, it.bcols] = total[:, :Q]

    def even4(it):
        wait(it, "z")
        gelu(it, zmine[it.g, :, :, it.bcols] + zr[it.g, :, :, it.bcols].astype(F32))
        start(it, ("Z", 1))

    def even9(it):
        start(it, ("Z", 0))

    def y_gather(it, a):
        wait(it, ("Z", a))
        start(it, ("Y+", a), ("Y-", a))

    def odd1(it):
        g, low, high, c = it.g, pl.ds(0, Q), pl.ds(Q, Q), it.cols
        core_wait(it)
        zsw[g, :, :, c] = (mine[g, :, high, c] + crecv[g, :, high, c].astype(F32)).astype(BF16)
        start(it, "z")
        mine[g, :, low, c] += crecv[g, :, low, c].astype(F32)

    def odd2(it):
        wait(it, "z")
        y_first(it, lambda dy: mine[it.g, :, pl.ds(0, Q), it.ycols(dy)] + zrw[it.g, :, :, it.ycols(dy)].astype(F32))

    def odd4(it):
        gelu(it, y_last(it))
        start(it, ("Y+", 1), ("Y-", 1))

    def odd9(it):
        start(it, ("Y+", 0), ("Y-", 0))

    def y_forward(it, a):
        wait(it, ("Y+", a))
        start(it, ("R+", a))
        wait(it, ("Y-", a))
        start(it, ("R-", a))

    def even_core(it, a):
        wait(it, ("R+", a), ("R-", a))
        start(it, ("C", a))

    def z_gather(it, a):
        wait(it, ("R+", a), ("R-", a))
        start(it, ("Z", a))

    def odd_core(it, a):
        wait(it, ("Z", a))
        start(it, ("C", a))

    def sent(it, names):
        for name in names:
            src, dst, _, send, recv, peer = item_copy(it, name)
            remote(src, dst, send, recv, peer).wait_send()

    def end(it):
        wait(it, ("C", 0))
        sent(it, [name for name in NAMES if name in SUMS or name[1] == 1])
        for f in range(it.f, it.f + it.n):
            core_copy(it.g, f * COLS).wait_send()

    def d_copy(i):
        return remote(dsend.at[i], drecv.at[i], d_send.at[i], d_recv.at[i], dp_peer(*dps[i]))

    summed = [0] * GROUPS

    def hidden_sum(it):
        wait(it, ("C", 1))

        def chunk(c0):
            cols = pl.ds(c0, COLS)
            acc[pl.ds(it.r0, R)] += dot_nt(ag[1, pl.ds(it.r0, R), cols], wi[:, cols])

        chunks(it, chunk)
        summed[it.g] += it.n
        if summed[it.g] == NF:
            for i, place in enumerate(dps):
                if place in PLACES[it.g]:
                    dsend[i] = acc[rows_from(*place)].astype(BF16)
                    d_copy(i).start()

    def grad_w_in(it):
        def chunk(c0):
            cols = pl.ds(c0, COLS)
            gwi_ref[:, cols] = (dot(xt[...], ag[1, :, cols]) * FACTOR).astype(BF16)

        chunks(it, chunk)

    def grad_w_out(it):
        def chunk(c0):
            cols = pl.ds(c0, COLS)
            gwo_ref[cols, :] = (dot_tn(ag[0, :, cols], xg[1]) * FACTOR).astype(BF16)

        chunks(it, chunk)

    acc[...] = jnp.zeros_like(acc)

    def of(stage, a):
        return lambda it: stage(it, a)

    tail = (end, grad_w_in, grad_w_out)
    stages = (
        (products, even1, y_relay, even3, even4, of(y_gather, 1), of(y_forward, 1), of(even_core, 1), hidden_sum)
        + (even9, of(y_gather, 0), of(y_forward, 0), of(even_core, 0)) + tail,
        (products, odd1, odd2, y_relay, odd4, of(y_forward, 1), of(z_gather, 1), of(odd_core, 1), hidden_sum)
        + (odd9, of(y_forward, 0), of(z_gather, 0), of(odd_core, 0)) + tail,
    )
    items = [Item(i) for i in range(len(ITEMS))]
    for i, n in ORDER:
        stages[items[i].odd][n](items[i])

    total = acc[own]
    for i in range(len(dps)):
        d_copy(i).wait_recv()
        total = total + drecv[i].astype(F32)
    in_ref[...] = total

    for i in range(len(dps)):
        a_copy(i)[0].wait_send()
        d_copy(i).wait_send()
    for it in items:
        sent(it, [name for name in GATHERS if name[1] == 0])


def store_kernel(done, in_ref, gwi_ref, gwo_ref, xg, ag, in_out, gwi_out, gwo_out, gwo, sem):
    head = pl.ds(0, done)
    copies = [
        pltpu.make_async_copy(gwo_ref, gwo_out.at[head], sem.at[2]),
        pltpu.make_async_copy(gwi_ref, gwi_out, sem.at[1]),
        pltpu.make_async_copy(in_ref, in_out, sem.at[0]),
    ]
    for c in copies:
        c.start()
    for i, c0 in enumerate(range(done, ag.shape[2], COLS)):
        cols = pl.ds(c0, COLS)
        gwo[i] = (dot_tn(ag[0, :, cols], xg[1]) * FACTOR).astype(BF16)
        copies.append(pltpu.make_async_copy(gwo.at[i], gwo_out.at[cols], sem.at[3 + i]))
        copies[-1].start()
    for c in copies:
        c.wait()


def local(inputs, out_grads, w_in, w_out):
    T, D = inputs.shape
    FF = w_in.shape[1]
    NF = FF // COLS
    R = NX * T
    H, Q, TOK, BF = R // 2, R // 4, GROUPS * R, FF // NY
    DPS = GROUPS * NX - 1
    done = FF - STORED_LATE * COLS
    vmem = pl.BlockSpec(memory_space=pltpu.VMEM)
    hbm = pl.BlockSpec(memory_space=pltpu.HBM)
    dma = pltpu.SemaphoreType.DMA
    G = GROUPS
    parts = pl.pallas_call(
        functools.partial(block_kernel, T, D, NF),
        out_shape=[
            pltpu.VMEM((T, D), F32),
            pltpu.VMEM((D, FF), BF16),
            pltpu.VMEM((done, D), BF16),
            pltpu.VMEM((2, TOK, D), BF16),
            pltpu.VMEM((2, TOK, FF), BF16),
        ],
        in_specs=[hbm] * 4,
        out_specs=[vmem] * 5,
        scratch_shapes=[
            pltpu.VMEM((D, TOK), BF16),
            pltpu.VMEM((D, FF), BF16),
            pltpu.VMEM((FF, D), BF16),
            pltpu.VMEM((TOK, D), F32),
            pltpu.VMEM((G, 2, H, FF), BF16),
            pltpu.VMEM((G, 2, H, FF), BF16),
            pltpu.VMEM((G, 2, H, FF), F32),
            *[pltpu.VMEM((G, 2, H, BF), BF16)] * 6,
            *[pltpu.VMEM((G, 2, H, BF), F32)] * 2,
            pltpu.VMEM((G, 2, Q, BF), F32),
            *[pltpu.VMEM((G, 2, Q, BF), BF16)] * 2,
            *[pltpu.VMEM((G, 2, Q, FF), BF16)] * 2,
            pltpu.VMEM((DPS, T, D), BF16),
            pltpu.VMEM((DPS, T, D), BF16),
            dma((2,)), dma((NF,)), dma((NF,)),
            dma((DPS,)), dma((DPS,)),
            dma((G * NF,)), dma((G * NF,)),
            dma((len(ITEMS), len(NAMES))), dma((len(ITEMS), len(NAMES))),
            dma((DPS,)), dma((DPS,)),
        ],
        compiler_params=pltpu.CompilerParams(
            collective_id=0, has_side_effects=True, vmem_limit_bytes=44 * 2**20
        ),
        name="ffn_backward",
    )(inputs, out_grads, w_in, w_out)
    return pl.pallas_call(
        functools.partial(store_kernel, done),
        out_shape=[
            jax.ShapeDtypeStruct((T, D), F32),
            jax.ShapeDtypeStruct((D, FF), BF16),
            jax.ShapeDtypeStruct((FF, D), BF16),
        ],
        in_specs=[vmem] * 5,
        out_specs=[hbm] * 3,
        scratch_shapes=[
            pltpu.VMEM((max(STORED_LATE, 1), COLS, D), BF16),
            dma((3 + STORED_LATE,)),
        ],
        compiler_params=pltpu.CompilerParams(vmem_limit_bytes=12 * 2**20),
        name="store_results",
    )(*parts)


def solution(mesh):
    return jax.shard_map(
        local,
        mesh=mesh,
        in_specs=(P("dp", "mp"), P("dp", "mp"), P("mp", "dp"), P("dp", "mp")),
        out_specs=(P("dp", "mp"), P("mp", "dp"), P("dp", "mp")),
        check_vma=False,
    )
```

```python
import functools
import math

import jax
import jax.numpy as jnp
from jax import lax
from jax.experimental import pallas as pl
from jax.experimental.pallas import tpu as pltpu
from jax.sharding import PartitionSpec as P

MESH = pl.DeviceIdType.MESH
F32, BF16 = jnp.float32, jnp.bfloat16

NX, NY = 4, 4
FACTOR = 1.0 / math.sqrt(256)
PLACES = (((0, 0), (1, 0), (3, 0), (0, 1)), ((2, 0), (1, 1), (3, 1), (2, 1)))
GROUPS = len(PLACES)
COLS = 512
ITEMS = (
    (0, 0, 2, 1),
    (0, 2, 3, 0),
    (0, 5, 2, 1),
    (0, 7, 2, 0),
    (1, 0, 2, 1),
    (1, 2, 2, 1),
    (1, 4, 2, 0),
    (1, 6, 2, 0),
    (1, 8, 1, 1),
)
ORDER = (
    (0, 0), (1, 0), (0, 1), (2, 0), (1, 1), (3, 0), (2, 1), (4, 0), (3, 1), (0, 2),
    (5, 0), (4, 1), (1, 2), (6, 0), (5, 1), (3, 2), (2, 2), (0, 3), (7, 0), (6, 1),
    (1, 3), (8, 0), (4, 2), (7, 1), (3, 3), (2, 3), (0, 4), (8, 1), (5, 2), (6, 2),
    (1, 4), (4, 3), (3, 4), (0, 9), (7, 2), (2, 4), (8, 2), (0, 5), (5, 3), (1, 5),
    (6, 3), (3, 5), (4, 4), (1, 9), (0, 10), (7, 3), (2, 5), (8, 3), (0, 6), (5, 4),
    (2, 9), (6, 4), (3, 9), (1, 10), (1, 6), (3, 6), (7, 4), (4, 5), (4, 9), (2, 6),
    (8, 4), (8, 9), (5, 5), (7, 9), (6, 9), (0, 7), (5, 9), (2, 10), (6, 5), (0, 11),
    (3, 10), (1, 11), (7, 5), (1, 7), (0, 8), (4, 6), (3, 7), (4, 10), (8, 5), (8, 10),
    (2, 7), (5, 6), (7, 10), (5, 10), (2, 11), (6, 10), (1, 8), (6, 6), (2, 8), (3, 11),
    (0, 12), (1, 12), (3, 8), (7, 6), (8, 6), (4, 7), (8, 11), (4, 11), (0, 13), (7, 11),
    (1, 13), (5, 11), (5, 7), (6, 11), (4, 8), (6, 7), (3, 12), (4, 14), (7, 7), (2, 12),
    (8, 7), (7, 12), (5, 8), (8, 12), (3, 13), (6, 12), (6, 8), (7, 8), (2, 13), (8, 8),
    (8, 13), (7, 13), (6, 13), (4, 12), (5, 14), (5, 12), (6, 14), (4, 13), (7, 14), (5, 13),
    (8, 14), (4, 15), (5, 15),
)
STORED_LATE = 5
SUMS = ("y+", "y-", "r+", "r-", "z")
GATHERS = tuple((name, a) for a in range(2) for name in ("Z", "Y+", "Y-", "R+", "R-", "C"))
NAMES = SUMS + GATHERS


def rem(a, b):
    return lax.rem(a, jnp.int32(b))


def div(a, b):
    return lax.div(a, jnp.int32(b))


def dot(a, b):
    return lax.dot_general(a, b, (((1,), (0,)), ((), ())), preferred_element_type=F32)


def dot_nt(a, b):
    return lax.dot_general(a, b, (((1,), (1,)), ((), ())), preferred_element_type=F32)


def dot_tn(a, b):
    return lax.dot_general(a, b, (((0,), (0,)), ((), ())), preferred_element_type=F32)


def gelu_parts(v):
    cumul = 0.5 * (1.0 + lax.erf(v * (1.0 / math.sqrt(2.0))))
    density = jnp.exp(-0.5 * v * v) * (1.0 / math.sqrt(2.0 * math.pi))
    return v * cumul, cumul + v * density


def block_kernel(
    T, D, NF,
    x_hbm, g_hbm, wi_hbm, wo_hbm,
    in_ref, gwi_ref, gwo_ref, xg, ag,
    xt, wi, wo, acc,
    csend, crecv, mine, yp, ym, yq, rp, rm, rq, yown, yrel, zmine, zs, zr, zsw, zrw, dsend, drecv,
    load_sem, wi_sem, wo_sem, a_send, a_recv, c_send, c_recv, i_send, i_recv, d_send, d_recv,
):
    R = NX * T
    H, Q = R // 2, R // 4
    dp, mp = lax.axis_index("dp"), lax.axis_index("mp")
    x, zhi = div(dp, 2), rem(dp, 2)
    zlo, y, core = div(mp, 8), rem(div(mp, 2), NY), rem(mp, 2)

    def rows_of(g, j):
        slot = rem(j // 2 + core, 2) * 2 + rem(j % 2 + zlo, 2)
        return pl.ds(pl.multiple_of(g * R + slot * T, T), T)

    def rows_from(dx, dz):
        for g, places in enumerate(PLACES):
            if (dx, dz) in places:
                return rows_of(g, places.index((dx, dz)))

    def mp_peer(dz=0, dy=0, dc=0):
        return (dp, rem(zlo + dz, 2) * 8 + rem(y + dy, NY) * 2 + rem(core + dc, 2))

    def dp_peer(dx, dz):
        return (rem(x + dx, NX) * 2 + rem(zhi + dz, 2), mp)

    peers = [mp_peer(dc=1), mp_peer(dz=1)] + [mp_peer(dy=k) for k in range(1, NY)]
    dps = [place for places in PLACES for place in places if place != (0, 0)]
    barrier = pltpu.get_barrier_semaphore()
    for peer in peers + [dp_peer(*place) for place in dps]:
        pl.semaphore_signal(barrier, inc=1, device_id=peer, device_id_type=MESH)

    own = rows_of(0, 0)
    loads = [
        pltpu.make_async_copy(x_hbm, xg.at[0, own], load_sem.at[0]),
        pltpu.make_async_copy(g_hbm, xg.at[1, own], load_sem.at[1]),
    ]
    for c in loads:
        c.start()

    def wi_copy(f):
        cols = pl.ds(f * COLS, COLS)
        return pltpu.make_async_copy(wi_hbm.at[:, cols], wi.at[:, cols], wi_sem.at[f])

    def wo_copy(f):
        rows = pl.ds(f * COLS, COLS)
        return pltpu.make_async_copy(wo_hbm.at[rows], wo.at[rows], wo_sem.at[f])

    for f in range(NF):
        wi_copy(f).start()
        wo_copy(f).start()

    def remote(src, dst, send, recv, peer):
        return pltpu.make_async_remote_copy(
            src_ref=src, dst_ref=dst, send_sem=send, recv_sem=recv, device_id=peer, device_id_type=MESH
        )

    def a_copy(i, a):
        dx, dz = dps[i]
        back = (-dx) % NX
        src = rows_from(0, 1) if dx and dz else own
        peer = dp_peer(dx, 0) if dx else dp_peer(0, dz)
        rows = rows_from(back, dz)
        sems = a_send.at[i, a], a_recv.at[i, a]
        return remote(xg.at[a, src], xg.at[a, rows], *sems, peer), remote(xg.at[a, rows], xg.at[a, rows], *sems, peer)

    def gather_start(*places):
        for a in range(2):
            for place in places:
                a_copy(dps.index(place), a)[0].start()

    def gather_wait(a, *places):
        for place in places:
            a_copy(dps.index(place), a)[1].wait_recv()

    near, partner = ((1, 0), (3, 0)), (0, 1)
    opposite, beyond = (2, 0), ((1, 1), (3, 1), (2, 1))

    for c in loads:
        c.wait()
    pl.semaphore_wait(barrier, len(peers) + len(dps))
    gather_start(*near, partner)

    class Item:
        def __init__(self, i):
            g, f, n, self.odd = ITEMS[i]
            self.i, self.g, self.f, self.n = i, g, f, n
            self.r0, self.c0, self.width = g * R, f * COLS, n * COLS
            self.block = self.width // NY
            self.cols = pl.ds(self.c0, self.width)
            self.bcols = pl.ds(self.c0 // NY, self.block)
            self.rows = Q if self.odd else H

        def ycols(self, dy):
            start = self.c0 + rem(y + dy, NY) * self.block
            return pl.ds(pl.multiple_of(start, 128), self.block)

    def item_copy(it, name):
        g, r0, bc, n = it.g, it.r0, it.bcols, NAMES.index(name)
        up, down, zp, cp = mp_peer(dy=1), mp_peer(dy=NY - 1), mp_peer(dz=1), mp_peer(dc=1)
        head, own_z, other_z, gather = pl.ds(0, it.rows), pl.ds(r0, Q), pl.ds(r0 + Q, Q), pl.ds(r0, it.rows)
        land = None
        if name == "y+":
            src, dst, peer = yp.at[g, :, head, bc], rp.at[g, :, head, bc], up
        elif name == "y-":
            src, dst, peer = ym.at[g, :, head, bc], rm.at[g, :, head, bc], down
        elif name == "r+":
            src, dst, peer = yq.at[g, 0, head, bc], rq.at[g, 0, head, bc], up
        elif name == "r-":
            src, dst, peer = yq.at[g, 1, head, bc], rq.at[g, 1, head, bc], down
        elif name == "z" and it.odd:
            src, dst, peer = zsw.at[g, :, :, it.cols], zrw.at[g, :, :, it.cols], zp
        elif name == "z":
            src, dst, peer = zs.at[g, :, :, bc], zr.at[g, :, :, bc], zp
        else:
            name, a = name
            half = it.rows // 2
            if name == "Z":
                zc = it.cols if it.odd else it.ycols(0)
                src, dst, peer = ag.at[a, own_z, zc], ag.at[a, other_z, zc], zp
            elif name == "Y+":
                src = dst = ag.at[a, gather, it.ycols(0)]
                land, peer = ag.at[a, gather, it.ycols(NY - 1)], up
            elif name == "Y-":
                src = dst = ag.at[a, gather, it.ycols(0)]
                land, peer = ag.at[a, gather, it.ycols(1)], down
            elif name == "R+":
                src = dst = ag.at[a, pl.ds(r0, half), it.ycols(NY - 1)]
                land, peer = ag.at[a, pl.ds(r0, half), it.ycols(2)], up
            elif name == "R-":
                src = dst = ag.at[a, pl.ds(r0 + half, half), it.ycols(1)]
                land, peer = ag.at[a, pl.ds(r0 + half, half), it.ycols(2)], down
            else:
                src, dst, peer = ag.at[a, pl.ds(r0, H), it.cols], ag.at[a, pl.ds(r0 + H, H), it.cols], cp
        land = dst if land is None else land
        send, recv = i_send.at[it.i, n], i_recv.at[it.i, n]
        return src, dst, land, send, recv, peer

    def start(it, *names):
        for name in names:
            src, dst, _, send, recv, peer = item_copy(it, name)
            remote(src, dst, send, recv, peer).start()

    def wait(it, *names):
        for name in names:
            _, _, land, send, recv, peer = item_copy(it, name)
            remote(land, land, send, recv, peer).wait_recv()

    def core_copy(g, c0):
        cols, n = pl.ds(c0, COLS), g * NF + c0 // COLS
        return remote(csend.at[g, :, :, cols], crecv.at[g, :, :, cols], c_send.at[n], c_recv.at[n], mp_peer(dc=1))

    def core_wait(it):
        for f in range(it.f, it.f + it.n):
            core_copy(it.g, f * COLS).wait_recv()

    def products(it):
        if it.i == 0:
            gather_wait(0, *near, partner)
        if it.g == 1 and it.f == 0:
            gather_wait(0, opposite, *beyond)
            gather_wait(1, opposite, *beyond)
            xt[...] = xg[0].T
        if it.g == 0:
            for f in range(it.f, it.f + it.n):
                wi_copy(f).wait()
                wo_copy(f).wait()

        def pre_chunk(c0):
            cols = pl.ds(c0, COLS)
            pre = dot(xg[0, pl.ds(it.r0, R)], wi[:, cols])
            mine[it.g, 0, :, cols] = pre[:H]
            csend[it.g, 0, :, cols] = pre[H:].astype(BF16)

        def grad_chunk(c0):
            cols = pl.ds(c0, COLS)
            grad = dot_nt(xg[1, pl.ds(it.r0, R)], wo[cols])
            mine[it.g, 1, :, cols] = grad[:H]
            csend[it.g, 1, :, cols] = grad[H:].astype(BF16)
            core_copy(it.g, c0).start()

        def chunk(c0):
            pre_chunk(c0)
            grad_chunk(c0)

        if it.i == 0:
            chunks(it, pre_chunk)
            gather_wait(1, *near, partner)
            gather_start(opposite, *beyond)
            chunks(it, grad_chunk)
        else:
            chunks(it, chunk)

    def chunks(it, run):
        if it.n == 1:
            run(it.c0)
        else:
            @pl.loop(0, it.n)
            def _(j):
                run(pl.multiple_of(it.c0 + j * COLS, COLS))

    def y_first(it, block):
        g, h, bc = it.g, pl.ds(0, it.rows), it.bcols
        b = block(2)
        yp[g, 0, h, bc] = b[0].astype(BF16)
        ym[g, 1, h, bc] = b[1].astype(BF16)
        b = block(1)
        yrel[g, 0, h, bc] = b[0]
        yp[g, 1, h, bc] = b[1].astype(BF16)
        start(it, "y+")
        b = block(3)
        yrel[g, 1, h, bc] = b[1]
        ym[g, 0, h, bc] = b[0].astype(BF16)
        start(it, "y-")
        yown[g, :, h, bc] = block(0)

    def y_relay(it):
        g, h, bc = it.g, pl.ds(0, it.rows), it.bcols
        wait(it, "y+")
        yq[g, 0, h, bc] = (yrel[g, 0, h, bc] + rp[g, 0, h, bc].astype(F32)).astype(BF16)
        start(it, "r+")
        wait(it, "y-")
        yq[g, 1, h, bc] = (yrel[g, 1, h, bc] + rm[g, 1, h, bc].astype(F32)).astype(BF16)
        start(it, "r-")
        yown[g, 0, h, bc] += rm[g, 0, h, bc].astype(F32)
        yown[g, 1, h, bc] += rp[g, 1, h, bc].astype(F32)

    def y_last(it):
        g, h, bc = it.g, pl.ds(0, it.rows), it.bcols
        wait(it, "r+", "r-")
        return yown[g, :, h, bc] + rq[g, :, h, bc].astype(F32)

    def gelu(it, total):
        value, slope = gelu_parts(total[0])
        ag[0, pl.ds(it.r0, Q), it.ycols(0)] = value.astype(BF16)
        ag[1, pl.ds(it.r0, Q), it.ycols(0)] = (total[1] * slope).astype(BF16)

    def even1(it):
        core_wait(it)
        y_first(it, lambda dy: mine[it.g, :, :, it.ycols(dy)] + crecv[it.g, :, :, it.ycols(dy)].astype(F32))

    def even3(it):
        total = y_last(it)
        zs[it.g, :, :, it.bcols] = total[:, Q:].astype(BF16)
        start(it, "z")
        zmine[it.g, :, :, it.bcols] = total[:, :Q]

    def even4(it):
        wait(it, "z")
        gelu(it, zmine[it.g, :, :, it.bcols] + zr[it.g, :, :, it.bcols].astype(F32))
        start(it, ("Z", 1))

    def even9(it):
        start(it, ("Z", 0))

    def y_gather(it, a):
        wait(it, ("Z", a))
        start(it, ("Y+", a), ("Y-", a))

    def odd1(it):
        g, low, high, c = it.g, pl.ds(0, Q), pl.ds(Q, Q), it.cols
        core_wait(it)
        zsw[g, :, :, c] = (mine[g, :, high, c] + crecv[g, :, high, c].astype(F32)).astype(BF16)
        start(it, "z")
        mine[g, :, low, c] += crecv[g, :, low, c].astype(F32)

    def odd2(it):
        wait(it, "z")
        y_first(it, lambda dy: mine[it.g, :, pl.ds(0, Q), it.ycols(dy)] + zrw[it.g, :, :, it.ycols(dy)].astype(F32))

    def odd4(it):
        gelu(it, y_last(it))
        start(it, ("Y+", 1), ("Y-", 1))

    def odd9(it):
        start(it, ("Y+", 0), ("Y-", 0))

    def y_forward(it, a):
        wait(it, ("Y+", a))
        start(it, ("R+", a))
        wait(it, ("Y-", a))
        start(it, ("R-", a))

    def even_core(it, a):
        wait(it, ("R+", a), ("R-", a))
        start(it, ("C", a))

    def z_gather(it, a):
        wait(it, ("R+", a), ("R-", a))
        start(it, ("Z", a))

    def odd_core(it, a):
        wait(it, ("Z", a))
        start(it, ("C", a))

    def sent(it, names):
        for name in names:
            src, dst, _, send, recv, peer = item_copy(it, name)
            remote(src, dst, send, recv, peer).wait_send()

    def end(it):
        wait(it, ("C", 0))
        sent(it, [name for name in NAMES if name in SUMS or name[1] == 1])
        for f in range(it.f, it.f + it.n):
            core_copy(it.g, f * COLS).wait_send()

    def d_copy(i):
        return remote(dsend.at[i], drecv.at[i], d_send.at[i], d_recv.at[i], dp_peer(*dps[i]))

    summed = [0] * GROUPS

    def hidden_sum(it):
        wait(it, ("C", 1))

        def chunk(c0):
            cols = pl.ds(c0, COLS)
            acc[pl.ds(it.r0, R)] += dot_nt(ag[1, pl.ds(it.r0, R), cols], wi[:, cols])

        chunks(it, chunk)
        summed[it.g] += it.n
        if summed[it.g] == NF:
            for i, place in enumerate(dps):
                if place in PLACES[it.g]:
                    dsend[i] = acc[rows_from(*place)].astype(BF16)
                    d_copy(i).start()

    def grad_w_in(it):
        def chunk(c0):
            cols = pl.ds(c0, COLS)
            gwi_ref[:, cols] = (dot(xt[...], ag[1, :, cols]) * FACTOR).astype(BF16)

        chunks(it, chunk)

    def grad_w_out(it):
        def chunk(c0):
            cols = pl.ds(c0, COLS)
            gwo_ref[cols, :] = (dot_tn(ag[0, :, cols], xg[1]) * FACTOR).astype(BF16)

        chunks(it, chunk)

    acc[...] = jnp.zeros_like(acc)

    def of(stage, a):
        return lambda it: stage(it, a)

    tail = (end, grad_w_in, grad_w_out)
    stages = (
        (products, even1, y_relay, even3, even4, of(y_gather, 1), of(y_forward, 1), of(even_core, 1), hidden_sum)
        + (even9, of(y_gather, 0), of(y_forward, 0), of(even_core, 0)) + tail,
        (products, odd1, odd2, y_relay, odd4, of(y_forward, 1), of(z_gather, 1), of(odd_core, 1), hidden_sum)
        + (odd9, of(y_forward, 0), of(z_gather, 0), of(odd_core, 0)) + tail,
    )
    items = [Item(i) for i in range(len(ITEMS))]
    for i, n in ORDER:
        stages[items[i].odd][n](items[i])

    total = acc[own]
    for i in range(len(dps)):
        d_copy(i).wait_recv()
        total = total + drecv[i].astype(F32)
    in_ref[...] = total

    for i in range(len(dps)):
        a_copy(i, 0)[0].wait_send()
        a_copy(i, 1)[0].wait_send()
        d_copy(i).wait_send()
    for it in items:
        sent(it, [name for name in GATHERS if name[1] == 0])


def store_kernel(done, in_ref, gwi_ref, gwo_ref, xg, ag, in_out, gwi_out, gwo_out, gwo, sem):
    head = pl.ds(0, done)
    copies = [
        pltpu.make_async_copy(gwo_ref, gwo_out.at[head], sem.at[2]),
        pltpu.make_async_copy(gwi_ref, gwi_out, sem.at[1]),
        pltpu.make_async_copy(in_ref, in_out, sem.at[0]),
    ]
    for c in copies:
        c.start()
    for i, c0 in enumerate(range(done, ag.shape[2], COLS)):
        cols = pl.ds(c0, COLS)
        gwo[i] = (dot_tn(ag[0, :, cols], xg[1]) * FACTOR).astype(BF16)
        copies.append(pltpu.make_async_copy(gwo.at[i], gwo_out.at[cols], sem.at[3 + i]))
        copies[-1].start()
    for c in copies:
        c.wait()


def local(inputs, out_grads, w_in, w_out):
    T, D = inputs.shape
    FF = w_in.shape[1]
    NF = FF // COLS
    R = NX * T
    H, Q, TOK, BF = R // 2, R // 4, GROUPS * R, FF // NY
    DPS = GROUPS * NX - 1
    done = FF - STORED_LATE * COLS
    vmem = pl.BlockSpec(memory_space=pltpu.VMEM)
    hbm = pl.BlockSpec(memory_space=pltpu.HBM)
    dma = pltpu.SemaphoreType.DMA
    G = GROUPS
    parts = pl.pallas_call(
        functools.partial(block_kernel, T, D, NF),
        out_shape=[
            pltpu.VMEM((T, D), F32),
            pltpu.VMEM((D, FF), BF16),
            pltpu.VMEM((done, D), BF16),
            pltpu.VMEM((2, TOK, D), BF16),
            pltpu.VMEM((2, TOK, FF), BF16),
        ],
        in_specs=[hbm] * 4,
        out_specs=[vmem] * 5,
        scratch_shapes=[
            pltpu.VMEM((D, TOK), BF16),
            pltpu.VMEM((D, FF), BF16),
            pltpu.VMEM((FF, D), BF16),
            pltpu.VMEM((TOK, D), F32),
            pltpu.VMEM((G, 2, H, FF), BF16),
            pltpu.VMEM((G, 2, H, FF), BF16),
            pltpu.VMEM((G, 2, H, FF), F32),
            *[pltpu.VMEM((G, 2, H, BF), BF16)] * 6,
            *[pltpu.VMEM((G, 2, H, BF), F32)] * 2,
            pltpu.VMEM((G, 2, Q, BF), F32),
            *[pltpu.VMEM((G, 2, Q, BF), BF16)] * 2,
            *[pltpu.VMEM((G, 2, Q, FF), BF16)] * 2,
            pltpu.VMEM((DPS, T, D), BF16),
            pltpu.VMEM((DPS, T, D), BF16),
            dma((2,)), dma((NF,)), dma((NF,)),
            dma((DPS, 2)), dma((DPS, 2)),
            dma((G * NF,)), dma((G * NF,)),
            dma((len(ITEMS), len(NAMES))), dma((len(ITEMS), len(NAMES))),
            dma((DPS,)), dma((DPS,)),
        ],
        compiler_params=pltpu.CompilerParams(
            collective_id=0, has_side_effects=True, vmem_limit_bytes=44 * 2**20
        ),
        name="ffn_backward",
    )(inputs, out_grads, w_in, w_out)
    return pl.pallas_call(
        functools.partial(store_kernel, done),
        out_shape=[
            jax.ShapeDtypeStruct((T, D), F32),
            jax.ShapeDtypeStruct((D, FF), BF16),
            jax.ShapeDtypeStruct((FF, D), BF16),
        ],
        in_specs=[vmem] * 5,
        out_specs=[hbm] * 3,
        scratch_shapes=[
            pltpu.VMEM((max(STORED_LATE, 1), COLS, D), BF16),
            dma((3 + STORED_LATE,)),
        ],
        compiler_params=pltpu.CompilerParams(vmem_limit_bytes=12 * 2**20),
        name="store_results",
    )(*parts)


def solution(mesh):
    return jax.shard_map(
        local,
        mesh=mesh,
        in_specs=(P("dp", "mp"), P("dp", "mp"), P("mp", "dp"), P("dp", "mp")),
        out_specs=(P("dp", "mp"), P("mp", "dp"), P("dp", "mp")),
        check_vma=False,
    )
```

```python
import functools
import math

import jax
import jax.numpy as jnp
from jax import lax
from jax.experimental import pallas as pl
from jax.experimental.pallas import tpu as pltpu
from jax.sharding import PartitionSpec as P

MESH = pl.DeviceIdType.MESH
F32, BF16 = jnp.float32, jnp.bfloat16

NX, NY = 4, 4
FACTOR = 1.0 / math.sqrt(256)
PLACES = (((0, 0), (1, 0), (3, 0), (0, 1)), ((2, 0), (1, 1), (3, 1), (2, 1)))
GROUPS = len(PLACES)
COLS = 512
ITEMS = (
    (0, 0, 2, 1),
    (0, 2, 3, 0),
    (0, 5, 2, 1),
    (0, 7, 2, 0),
    (1, 0, 2, 1),
    (1, 2, 2, 1),
    (1, 4, 2, 0),
    (1, 6, 2, 0),
    (1, 8, 1, 1),
)
ORDER = (
    (0, 0), (1, 0), (0, 1), (2, 0), (1, 1), (3, 0), (2, 1), (4, 0), (3, 1), (0, 2),
    (5, 0), (4, 1), (1, 2), (6, 0), (5, 1), (3, 2), (2, 2), (0, 3), (7, 0), (6, 1),
    (1, 3), (8, 0), (4, 2), (7, 1), (3, 3), (2, 3), (0, 4), (8, 1), (5, 2), (6, 2),
    (1, 4), (4, 3), (3, 4), (0, 9), (7, 2), (2, 4), (8, 2), (0, 5), (5, 3), (1, 5),
    (6, 3), (3, 5), (4, 4), (1, 9), (0, 10), (7, 3), (2, 5), (8, 3), (0, 6), (5, 4),
    (2, 9), (6, 4), (3, 9), (1, 10), (1, 6), (3, 6), (7, 4), (4, 5), (4, 9), (2, 6),
    (8, 4), (8, 9), (5, 5), (7, 9), (6, 9), (0, 7), (5, 9), (2, 10), (6, 5), (0, 11),
    (3, 10), (1, 11), (7, 5), (1, 7), (0, 8), (4, 6), (3, 7), (4, 10), (8, 5), (8, 10),
    (2, 7), (5, 6), (7, 10), (5, 10), (2, 11), (6, 10), (1, 8), (6, 6), (2, 8), (3, 11),
    (0, 12), (1, 12), (3, 8), (7, 6), (8, 6), (4, 7), (8, 11), (4, 11), (0, 13), (7, 11),
    (1, 13), (5, 11), (5, 7), (6, 11), (4, 8), (6, 7), (3, 12), (4, 14), (7, 7), (2, 12),
    (8, 7), (7, 12), (5, 8), (8, 12), (3, 13), (6, 12), (6, 8), (7, 8), (2, 13), (8, 8),
    (8, 13), (7, 13), (6, 13), (4, 12), (5, 14), (5, 12), (6, 14), (4, 13), (7, 14), (5, 13),
    (8, 14), (4, 15), (5, 15),
)
STORED_LATE = 5
SUMS = ("y+", "y-", "r+", "r-", "z")
GATHERS = tuple((name, a) for a in range(2) for name in ("Z", "Y+", "Y-", "R+", "R-", "C"))
NAMES = SUMS + GATHERS


def rem(a, b):
    return lax.rem(a, jnp.int32(b))


def div(a, b):
    return lax.div(a, jnp.int32(b))


def dot(a, b):
    return lax.dot_general(a, b, (((1,), (0,)), ((), ())), preferred_element_type=F32)


def dot_nt(a, b):
    return lax.dot_general(a, b, (((1,), (1,)), ((), ())), preferred_element_type=F32)


def dot_tn(a, b):
    return lax.dot_general(a, b, (((0,), (0,)), ((), ())), preferred_element_type=F32)


def gelu_parts(v):
    cumul = 0.5 * (1.0 + lax.erf(v * (1.0 / math.sqrt(2.0))))
    density = jnp.exp(-0.5 * v * v) * (1.0 / math.sqrt(2.0 * math.pi))
    return v * cumul, cumul + v * density


def block_kernel(
    T, D, NF,
    x_hbm, g_hbm, wi_hbm, wo_hbm,
    in_ref, gwi_ref, gwo_ref, xg, ag,
    xt, wi, wo, acc,
    csend, crecv, mine, yp, ym, yq, rp, rm, rq, yown, yrel, zmine, zs, zr, zsw, zrw, dsend, drecv,
    load_sem, wi_sem, wo_sem, a_send, a_recv, c_send, c_recv, i_send, i_recv, d_send, d_recv,
):
    R = NX * T
    H, Q = R // 2, R // 4
    dp, mp = lax.axis_index("dp"), lax.axis_index("mp")
    x, zhi = div(dp, 2), rem(dp, 2)
    zlo, y, core = div(mp, 8), rem(div(mp, 2), NY), rem(mp, 2)

    def rows_of(g, j):
        slot = rem(j // 2 + core, 2) * 2 + rem(j % 2 + zlo, 2)
        return pl.ds(pl.multiple_of(g * R + slot * T, T), T)

    def rows_from(dx, dz):
        for g, places in enumerate(PLACES):
            if (dx, dz) in places:
                return rows_of(g, places.index((dx, dz)))

    def mp_peer(dz=0, dy=0, dc=0):
        return (dp, rem(zlo + dz, 2) * 8 + rem(y + dy, NY) * 2 + rem(core + dc, 2))

    def dp_peer(dx, dz):
        return (rem(x + dx, NX) * 2 + rem(zhi + dz, 2), mp)

    dps = [place for places in PLACES for place in places if place != (0, 0)]
    near, partner = ((1, 0), (3, 0)), (0, 1)
    opposite, beyond = (2, 0), ((1, 1), (3, 1), (2, 1))
    peers = [mp_peer(dc=1), mp_peer(dz=1), mp_peer(dy=1), mp_peer(dy=NY - 1)] + [dp_peer(*p) for p in (*near, partner)]
    barrier = pltpu.get_barrier_semaphore()
    for peer in peers:
        pl.semaphore_signal(barrier, inc=1, device_id=peer, device_id_type=MESH)

    own = rows_of(0, 0)
    loads = [
        pltpu.make_async_copy(x_hbm, xg.at[0, own], load_sem.at[0]),
        pltpu.make_async_copy(g_hbm, xg.at[1, own], load_sem.at[1]),
    ]
    for c in loads:
        c.start()

    def wi_copy(f):
        cols = pl.ds(f * COLS, COLS)
        return pltpu.make_async_copy(wi_hbm.at[:, cols], wi.at[:, cols], wi_sem.at[f])

    def wo_copy(f):
        rows = pl.ds(f * COLS, COLS)
        return pltpu.make_async_copy(wo_hbm.at[rows], wo.at[rows], wo_sem.at[f])

    for f in range(NF):
        wi_copy(f).start()
        wo_copy(f).start()

    def remote(src, dst, send, recv, peer):
        return pltpu.make_async_remote_copy(
            src_ref=src, dst_ref=dst, send_sem=send, recv_sem=recv, device_id=peer, device_id_type=MESH
        )

    def a_copy(i, a):
        dx, dz = dps[i]
        back = (-dx) % NX
        src = rows_from(0, 1) if dx and dz else own
        peer = dp_peer(dx, 0) if dx else dp_peer(0, dz)
        rows = rows_from(back, dz)
        sems = a_send.at[i, a], a_recv.at[i, a]
        return remote(xg.at[a, src], xg.at[a, rows], *sems, peer), remote(xg.at[a, rows], xg.at[a, rows], *sems, peer)

    def gather_start(*places):
        for a in range(2):
            for place in places:
                a_copy(dps.index(place), a)[0].start()

    def gather_wait(a, *places):
        for place in places:
            a_copy(dps.index(place), a)[1].wait_recv()

    for c in loads:
        c.wait()
    pl.semaphore_wait(barrier, len(peers))
    gather_start(*near, partner)

    class Item:
        def __init__(self, i):
            g, f, n, self.odd = ITEMS[i]
            self.i, self.g, self.f, self.n = i, g, f, n
            self.r0, self.c0, self.width = g * R, f * COLS, n * COLS
            self.block = self.width // NY
            self.cols = pl.ds(self.c0, self.width)
            self.bcols = pl.ds(self.c0 // NY, self.block)
            self.rows = Q if self.odd else H

        def ycols(self, dy):
            start = self.c0 + rem(y + dy, NY) * self.block
            return pl.ds(pl.multiple_of(start, 128), self.block)

    def item_copy(it, name):
        g, r0, bc, n = it.g, it.r0, it.bcols, NAMES.index(name)
        up, down, zp, cp = mp_peer(dy=1), mp_peer(dy=NY - 1), mp_peer(dz=1), mp_peer(dc=1)
        head, own_z, other_z, gather = pl.ds(0, it.rows), pl.ds(r0, Q), pl.ds(r0 + Q, Q), pl.ds(r0, it.rows)
        land = None
        if name == "y+":
            src, dst, peer = yp.at[g, :, head, bc], rp.at[g, :, head, bc], up
        elif name == "y-":
            src, dst, peer = ym.at[g, :, head, bc], rm.at[g, :, head, bc], down
        elif name == "r+":
            src, dst, peer = yq.at[g, 0, head, bc], rq.at[g, 0, head, bc], up
        elif name == "r-":
            src, dst, peer = yq.at[g, 1, head, bc], rq.at[g, 1, head, bc], down
        elif name == "z" and it.odd:
            src, dst, peer = zsw.at[g, :, :, it.cols], zrw.at[g, :, :, it.cols], zp
        elif name == "z":
            src, dst, peer = zs.at[g, :, :, bc], zr.at[g, :, :, bc], zp
        else:
            name, a = name
            half = it.rows // 2
            if name == "Z":
                zc = it.cols if it.odd else it.ycols(0)
                src, dst, peer = ag.at[a, own_z, zc], ag.at[a, other_z, zc], zp
            elif name == "Y+":
                src = dst = ag.at[a, gather, it.ycols(0)]
                land, peer = ag.at[a, gather, it.ycols(NY - 1)], up
            elif name == "Y-":
                src = dst = ag.at[a, gather, it.ycols(0)]
                land, peer = ag.at[a, gather, it.ycols(1)], down
            elif name == "R+":
                src = dst = ag.at[a, pl.ds(r0, half), it.ycols(NY - 1)]
                land, peer = ag.at[a, pl.ds(r0, half), it.ycols(2)], up
            elif name == "R-":
                src = dst = ag.at[a, pl.ds(r0 + half, half), it.ycols(1)]
                land, peer = ag.at[a, pl.ds(r0 + half, half), it.ycols(2)], down
            else:
                src, dst, peer = ag.at[a, pl.ds(r0, H), it.cols], ag.at[a, pl.ds(r0 + H, H), it.cols], cp
        land = dst if land is None else land
        send, recv = i_send.at[it.i, n], i_recv.at[it.i, n]
        return src, dst, land, send, recv, peer

    def start(it, *names):
        for name in names:
            src, dst, _, send, recv, peer = item_copy(it, name)
            remote(src, dst, send, recv, peer).start()

    def wait(it, *names):
        for name in names:
            _, _, land, send, recv, peer = item_copy(it, name)
            remote(land, land, send, recv, peer).wait_recv()

    def core_copy(g, c0):
        cols, n = pl.ds(c0, COLS), g * NF + c0 // COLS
        return remote(csend.at[g, :, :, cols], crecv.at[g, :, :, cols], c_send.at[n], c_recv.at[n], mp_peer(dc=1))

    def core_wait(it):
        for f in range(it.f, it.f + it.n):
            core_copy(it.g, f * COLS).wait_recv()

    def products(it):
        if it.i == 0:
            gather_wait(0, *near, partner)
        if it.g == 1 and it.f == 0:
            gather_wait(0, opposite, *beyond)
            gather_wait(1, opposite, *beyond)
            xt[...] = xg[0].T
        if it.g == 0:
            for f in range(it.f, it.f + it.n):
                wi_copy(f).wait()
                wo_copy(f).wait()

        def pre_chunk(c0):
            cols = pl.ds(c0, COLS)
            pre = dot(xg[0, pl.ds(it.r0, R)], wi[:, cols])
            mine[it.g, 0, :, cols] = pre[:H]
            csend[it.g, 0, :, cols] = pre[H:].astype(BF16)

        def grad_chunk(c0):
            cols = pl.ds(c0, COLS)
            grad = dot_nt(xg[1, pl.ds(it.r0, R)], wo[cols])
            mine[it.g, 1, :, cols] = grad[:H]
            csend[it.g, 1, :, cols] = grad[H:].astype(BF16)
            core_copy(it.g, c0).start()

        def chunk(c0):
            pre_chunk(c0)
            grad_chunk(c0)

        if it.i == 0:
            chunks(it, pre_chunk)
            gather_wait(1, *near, partner)
            gather_start(opposite, *beyond)
            chunks(it, grad_chunk)
        else:
            chunks(it, chunk)

    def chunks(it, run):
        if it.n == 1:
            run(it.c0)
        else:
            @pl.loop(0, it.n)
            def _(j):
                run(pl.multiple_of(it.c0 + j * COLS, COLS))

    def y_first(it, block):
        g, h, bc = it.g, pl.ds(0, it.rows), it.bcols
        b = block(2)
        yp[g, 0, h, bc] = b[0].astype(BF16)
        ym[g, 1, h, bc] = b[1].astype(BF16)
        b = block(1)
        yrel[g, 0, h, bc] = b[0]
        yp[g, 1, h, bc] = b[1].astype(BF16)
        start(it, "y+")
        b = block(3)
        yrel[g, 1, h, bc] = b[1]
        ym[g, 0, h, bc] = b[0].astype(BF16)
        start(it, "y-")
        yown[g, :, h, bc] = block(0)

    def y_relay(it):
        g, h, bc = it.g, pl.ds(0, it.rows), it.bcols
        wait(it, "y+")
        yq[g, 0, h, bc] = (yrel[g, 0, h, bc] + rp[g, 0, h, bc].astype(F32)).astype(BF16)
        start(it, "r+")
        wait(it, "y-")
        yq[g, 1, h, bc] = (yrel[g, 1, h, bc] + rm[g, 1, h, bc].astype(F32)).astype(BF16)
        start(it, "r-")
        yown[g, 0, h, bc] += rm[g, 0, h, bc].astype(F32)
        yown[g, 1, h, bc] += rp[g, 1, h, bc].astype(F32)

    def y_last(it):
        g, h, bc = it.g, pl.ds(0, it.rows), it.bcols
        wait(it, "r+", "r-")
        return yown[g, :, h, bc] + rq[g, :, h, bc].astype(F32)

    def gelu(it, total):
        value, slope = gelu_parts(total[0])
        ag[0, pl.ds(it.r0, Q), it.ycols(0)] = value.astype(BF16)
        ag[1, pl.ds(it.r0, Q), it.ycols(0)] = (total[1] * slope).astype(BF16)

    def even1(it):
        core_wait(it)
        y_first(it, lambda dy: mine[it.g, :, :, it.ycols(dy)] + crecv[it.g, :, :, it.ycols(dy)].astype(F32))

    def even3(it):
        total = y_last(it)
        zs[it.g, :, :, it.bcols] = total[:, Q:].astype(BF16)
        start(it, "z")
        zmine[it.g, :, :, it.bcols] = total[:, :Q]

    def even4(it):
        wait(it, "z")
        gelu(it, zmine[it.g, :, :, it.bcols] + zr[it.g, :, :, it.bcols].astype(F32))
        start(it, ("Z", 1))

    def even9(it):
        start(it, ("Z", 0))

    def y_gather(it, a):
        wait(it, ("Z", a))
        start(it, ("Y+", a), ("Y-", a))

    def odd1(it):
        g, low, high, c = it.g, pl.ds(0, Q), pl.ds(Q, Q), it.cols
        core_wait(it)
        zsw[g, :, :, c] = (mine[g, :, high, c] + crecv[g, :, high, c].astype(F32)).astype(BF16)
        start(it, "z")
        mine[g, :, low, c] += crecv[g, :, low, c].astype(F32)

    def odd2(it):
        wait(it, "z")
        y_first(it, lambda dy: mine[it.g, :, pl.ds(0, Q), it.ycols(dy)] + zrw[it.g, :, :, it.ycols(dy)].astype(F32))

    def odd4(it):
        gelu(it, y_last(it))
        start(it, ("Y+", 1), ("Y-", 1))

    def odd9(it):
        start(it, ("Y+", 0), ("Y-", 0))

    def y_forward(it, a):
        wait(it, ("Y+", a))
        start(it, ("R+", a))
        wait(it, ("Y-", a))
        start(it, ("R-", a))

    def even_core(it, a):
        wait(it, ("R+", a), ("R-", a))
        start(it, ("C", a))

    def z_gather(it, a):
        wait(it, ("R+", a), ("R-", a))
        start(it, ("Z", a))

    def odd_core(it, a):
        wait(it, ("Z", a))
        start(it, ("C", a))

    def sent(it, names):
        for name in names:
            src, dst, _, send, recv, peer = item_copy(it, name)
            remote(src, dst, send, recv, peer).wait_send()

    def end(it):
        wait(it, ("C", 0))
        sent(it, [name for name in NAMES if name in SUMS or name[1] == 1])
        for f in range(it.f, it.f + it.n):
            core_copy(it.g, f * COLS).wait_send()

    def d_copy(i):
        return remote(dsend.at[i], drecv.at[i], d_send.at[i], d_recv.at[i], dp_peer(*dps[i]))

    summed = [0] * GROUPS

    def hidden_sum(it):
        wait(it, ("C", 1))

        def chunk(c0):
            cols = pl.ds(c0, COLS)
            acc[pl.ds(it.r0, R)] += dot_nt(ag[1, pl.ds(it.r0, R), cols], wi[:, cols])

        chunks(it, chunk)
        summed[it.g] += it.n
        if summed[it.g] == NF:
            for i, place in enumerate(dps):
                if place in PLACES[it.g]:
                    dsend[i] = acc[rows_from(*place)].astype(BF16)
                    d_copy(i).start()

    def grad_w_in(it):
        def chunk(c0):
            cols = pl.ds(c0, COLS)
            gwi_ref[:, cols] = (dot(xt[...], ag[1, :, cols]) * FACTOR).astype(BF16)

        chunks(it, chunk)

    def grad_w_out(it):
        def chunk(c0):
            cols = pl.ds(c0, COLS)
            gwo_ref[cols, :] = (dot_tn(ag[0, :, cols], xg[1]) * FACTOR).astype(BF16)

        chunks(it, chunk)

    acc[...] = jnp.zeros_like(acc)

    def of(stage, a):
        return lambda it: stage(it, a)

    tail = (end, grad_w_in, grad_w_out)
    stages = (
        (products, even1, y_relay, even3, even4, of(y_gather, 1), of(y_forward, 1), of(even_core, 1), hidden_sum)
        + (even9, of(y_gather, 0), of(y_forward, 0), of(even_core, 0)) + tail,
        (products, odd1, odd2, y_relay, odd4, of(y_forward, 1), of(z_gather, 1), of(odd_core, 1), hidden_sum)
        + (odd9, of(y_forward, 0), of(z_gather, 0), of(odd_core, 0)) + tail,
    )
    items = [Item(i) for i in range(len(ITEMS))]
    for i, n in ORDER:
        stages[items[i].odd][n](items[i])

    total = acc[own]
    for i in range(len(dps)):
        d_copy(i).wait_recv()
        total = total + drecv[i].astype(F32)
    in_ref[...] = total

    for i in range(len(dps)):
        a_copy(i, 0)[0].wait_send()
        a_copy(i, 1)[0].wait_send()
        d_copy(i).wait_send()
    for it in items:
        sent(it, [name for name in GATHERS if name[1] == 0])


def store_kernel(done, in_ref, gwi_ref, gwo_ref, xg, ag, in_out, gwi_out, gwo_out, gwo, sem):
    head = pl.ds(0, done)
    copies = [
        pltpu.make_async_copy(gwo_ref, gwo_out.at[head], sem.at[2]),
        pltpu.make_async_copy(gwi_ref, gwi_out, sem.at[1]),
        pltpu.make_async_copy(in_ref, in_out, sem.at[0]),
    ]
    for c in copies:
        c.start()
    for i, c0 in enumerate(range(done, ag.shape[2], COLS)):
        cols = pl.ds(c0, COLS)
        gwo[i] = (dot_tn(ag[0, :, cols], xg[1]) * FACTOR).astype(BF16)
        copies.append(pltpu.make_async_copy(gwo.at[i], gwo_out.at[cols], sem.at[3 + i]))
        copies[-1].start()
    for c in copies:
        c.wait()


def local(inputs, out_grads, w_in, w_out):
    T, D = inputs.shape
    FF = w_in.shape[1]
    NF = FF // COLS
    R = NX * T
    H, Q, TOK, BF = R // 2, R // 4, GROUPS * R, FF // NY
    DPS = GROUPS * NX - 1
    done = FF - STORED_LATE * COLS
    vmem = pl.BlockSpec(memory_space=pltpu.VMEM)
    hbm = pl.BlockSpec(memory_space=pltpu.HBM)
    dma = pltpu.SemaphoreType.DMA
    G = GROUPS
    parts = pl.pallas_call(
        functools.partial(block_kernel, T, D, NF),
        out_shape=[
            pltpu.VMEM((T, D), F32),
            pltpu.VMEM((D, FF), BF16),
            pltpu.VMEM((done, D), BF16),
            pltpu.VMEM((2, TOK, D), BF16),
            pltpu.VMEM((2, TOK, FF), BF16),
        ],
        in_specs=[hbm] * 4,
        out_specs=[vmem] * 5,
        scratch_shapes=[
            pltpu.VMEM((D, TOK), BF16),
            pltpu.VMEM((D, FF), BF16),
            pltpu.VMEM((FF, D), BF16),
            pltpu.VMEM((TOK, D), F32),
            pltpu.VMEM((G, 2, H, FF), BF16),
            pltpu.VMEM((G, 2, H, FF), BF16),
            pltpu.VMEM((G, 2, H, FF), F32),
            *[pltpu.VMEM((G, 2, H, BF), BF16)] * 6,
            *[pltpu.VMEM((G, 2, H, BF), F32)] * 2,
            pltpu.VMEM((G, 2, Q, BF), F32),
            *[pltpu.VMEM((G, 2, Q, BF), BF16)] * 2,
            *[pltpu.VMEM((G, 2, Q, FF), BF16)] * 2,
            pltpu.VMEM((DPS, T, D), BF16),
            pltpu.VMEM((DPS, T, D), BF16),
            dma((2,)), dma((NF,)), dma((NF,)),
            dma((DPS, 2)), dma((DPS, 2)),
            dma((G * NF,)), dma((G * NF,)),
            dma((len(ITEMS), len(NAMES))), dma((len(ITEMS), len(NAMES))),
            dma((DPS,)), dma((DPS,)),
        ],
        compiler_params=pltpu.CompilerParams(
            collective_id=0, has_side_effects=True, vmem_limit_bytes=44 * 2**20
        ),
        name="ffn_backward",
    )(inputs, out_grads, w_in, w_out)
    return pl.pallas_call(
        functools.partial(store_kernel, done),
        out_shape=[
            jax.ShapeDtypeStruct((T, D), F32),
            jax.ShapeDtypeStruct((D, FF), BF16),
            jax.ShapeDtypeStruct((FF, D), BF16),
        ],
        in_specs=[vmem] * 5,
        out_specs=[hbm] * 3,
        scratch_shapes=[
            pltpu.VMEM((max(STORED_LATE, 1), COLS, D), BF16),
            dma((3 + STORED_LATE,)),
        ],
        compiler_params=pltpu.CompilerParams(vmem_limit_bytes=12 * 2**20),
        name="store_results",
    )(*parts)


def solution(mesh):
    return jax.shard_map(
        local,
        mesh=mesh,
        in_specs=(P("dp", "mp"), P("dp", "mp"), P("mp", "dp"), P("dp", "mp")),
        out_specs=(P("dp", "mp"), P("mp", "dp"), P("dp", "mp")),
        check_vma=False,
    )
```
